256 devices in a mesh: dp: 64 (over y, z, x_lo), width: 4 (over x_hi, core).
Axes of the slice: x: 4 (x_hi: 2, x_lo: 2; x = x_hi * 2 + x_lo), y: 4, z: 8, core: 2. Of those that a mesh axis runs over, the one named last changes fastest.
Arguments:
- queries: bfloat16 [5632, 4096], P('dp', 'width'), may hold values from -12 to 12
- passages: bfloat16 [5632, 4096], P('dp', 'width'), may hold values from -12 to 12
- negatives: bfloat16 [5632, 4096], P('dp', 'width'), may hold values from -6 to 6
- neg_owner: int32 [5632, 7], P('dp'), may hold values from 0 to 63, all different within a row; in each aligned block of 88 rows (0 to 87, 88 to 175, ...) at most 19 rows name the same one
- neg_row: int32 [5632, 7], P('dp'), may hold values from 0 to 87
Outputs:
- row_loss: float32 [5632], P('dp')
- grad_queries: bfloat16 [5632, 4096], P('dp', 'width')
- grad_passages: bfloat16 [5632, 4096], P('dp', 'width')
- grad_negatives: bfloat16 [5632, 4096], P('dp', 'width')
The draws below stay inside these ranges and needn't reach their ends.
Inputs may be any that keep to these rules, and one draw needn't show every extreme that they name: `neg_owner`: the 7 owners of one query differ. Among the queries of one device, no owner is named more than 19 times, a bound that some block reaches.
All inputs are finite; a program needn't handle non-finite values.
Results may differ from the reference program's by a relative error of at most 0.0049.
Values may be sent and summed in bfloat16 or wider, within the bound.
No kernel may reach another device: no remote copies, remote signals or barrier semaphores. Data moves between devices by JAX's collectives and lax.ppermute only.
A program may use at most 128 MiB of HBM per device.

```python
import math
import jax
import jax.numpy as jnp
import numpy as np
from jax import lax

D = 4096
B_DEV = 88
NEG = 7
B = 5632
CAP = 19
N_DP = 64


def pair_fields(key, lift):
    first = jax.random.normal(jax.random.fold_in(key, 11), (B, D), jnp.float32)
    second = jax.random.normal(jax.random.fold_in(key, 12), (B, D), jnp.float32)
    row_ids = jnp.arange(B, dtype=jnp.int32)[:, None]
    strength = 1.3 + 0.7 * (row_ids // 64 % 4).astype(jnp.float32) / 3.0
    chosen = jnp.logical_and(row_ids % 64 == 7, lift > 0.0)
    query_values = jnp.where(chosen, strength * first, first)
    drawn_values = 0.1 * first + second
    passage_values = jnp.where(chosen, strength * first, drawn_values)
    offset = B // 2 + 32
    moved_first = jnp.roll(first, offset, axis=0)
    moved_strength = jnp.roll(strength, offset, axis=0)
    moved_chosen = jnp.roll(chosen, offset, axis=0)
    partner = moved_strength * (1.0 - 2.0 / (moved_strength * moved_strength * D ** 0.5)) * moved_first + 0.05 * second
    passage_values = jnp.where(moved_chosen, partner, passage_values)
    return (jnp.clip(query_values, -12.0, 12.0), jnp.clip(passage_values, -12.0, 12.0))


def draw_queries(key, part):
    fields = pair_fields(key, 0.0)
    return fields[0].astype(jnp.bfloat16)


def draw_passages(key, part):
    fields = pair_fields(key, 0.0)
    return fields[1].astype(jnp.bfloat16)


def touch_ends(drawn, own_key, least, top_value):
    place = [jax.random.randint(jax.random.fold_in(own_key, axis), (), 0, length) for axis, length in enumerate(drawn.shape)]
    widest = drawn.shape.index(max(drawn.shape))
    next_to = place[:widest] + [(place[widest] + 1) % drawn.shape[widest]] + place[widest + 1:]
    return drawn.at[tuple(place)].set(least).at[tuple(next_to)].set(top_value)


def shard_levels(key, shape, cuts, low, largest):
    factor_of = 1.0
    for axis_at, blocks in cuts:
        heights = jax.random.uniform(jax.random.fold_in(jax.random.fold_in(key, 6), axis_at), (blocks,), jnp.float32, low / len(cuts), largest / len(cuts))
        factor_of = factor_of * jnp.repeat(jnp.exp(heights), shape[axis_at] // blocks).reshape((-1,) + (1,) * (len(shape) - 1 - axis_at))
    return factor_of


def shared_out(rng, own, number, rows, number_of, top, reach, lean):
    sequence = jax.random.permutation(rng, number_of)
    packed, usual = shares(number_of, rows * top, reach, lean, True), shares(number_of, rows * top, reach, lean, False)
    places = jnp.arange(number_of)

    def named(tallies, rotation):
        used = int((tallies > 0).sum())
        fixed = max(1, used // 4)
        shifted = fixed + (places - fixed + rotation * (used - fixed)) % max(1, number_of - fixed)
        return jnp.zeros((number_of,), jnp.int32).at[sequence[jnp.where(places < fixed, places, shifted)]].set(jnp.asarray(tallies, jnp.int32))

    tallies = jnp.where(number % 4 == 0, named(packed, number // 4), named(usual, number - number // 4 - 1))
    mixed = jax.random.permutation(jax.random.fold_in(own, 3), number_of)
    source_of, taker = mixed[0:number_of // 2 * 2:2], mixed[1:number_of // 2 * 2:2]
    slack = jnp.minimum(tallies[source_of] - 1, reach - tallies[taker]) // 2
    slack = jnp.where((source_of == sequence[0]) | (taker == sequence[0]) | (tallies[taker] == 0), 0, jnp.maximum(slack, 0))
    shifted = jax.random.randint(jax.random.fold_in(own, 4), (number_of // 2,), 0, 1 << 20) % (slack + 1)
    tallies = tallies.at[source_of].add(-shifted).at[taker].add(shifted)
    items = jnp.searchsorted(jnp.cumsum(tallies), jnp.arange(rows * top), side="right").astype(jnp.int32)
    table = items.reshape(top, rows).T
    table = table[jax.random.permutation(jax.random.fold_in(own, 1), rows)]
    rotation = jax.random.randint(jax.random.fold_in(own, 2), (rows, 1), 0, top)
    return jnp.take_along_axis(table, (jnp.arange(top)[None, :] + rotation) % top, axis=1)


def shares(number_of, total, reach, skew, full):
    loads = [(1 << 20) // math.isqrt(rank ** skew) + 1 for rank in range(1, number_of + 1)]
    largest = reach if full else min(reach, max(-(-total // number_of), total * loads[0] // sum(loads)))
    least = 1 if total - largest >= number_of - 1 else 0
    holding, rest = [largest] + [least] * (number_of - 1), total - largest - least * (number_of - 1)
    while rest > 0:
        free = [i for i in range(1, number_of) if holding[i] < largest] or [i for i in range(1, number_of) if holding[i] < reach]
        whole, budget = sum([loads[i] for i in free]), rest
        for i in free:
            extra = min(reach - holding[i], max(1, budget * loads[i] // whole), rest)
            holding[i] = holding[i] + extra
            rest = rest - extra
    return np.array(holding)


def gaussian(stream_key, dims, width, most, shards=(), held_as=jnp.bfloat16):
    loudness = shard_levels(stream_key, dims, shards, -0.22, 0.18) if shards else 1.0
    entries = jax.random.normal(stream_key, dims, jnp.float32) * width * loudness
    return jnp.minimum(jnp.maximum(entries, -most), most).astype(held_as)


def setup_inputs(seed: int = 0) -> dict:
    streams_of = jax.random.split(jax.random.key(seed), 6)
    queries = draw_queries(jax.random.fold_in(streams_of[5], 71), 0)
    passages = draw_passages(jax.random.fold_in(streams_of[5], 71), 0)
    negatives = gaussian(streams_of[2], (B, D), 1.0, 6.0, ((0, 64), (1, 4)))
    neg_owner_keys = jax.random.split(jax.random.fold_in(streams_of[3], 1), B // B_DEV)
    neg_owner_turns = jax.random.permutation(jax.random.fold_in(streams_of[3], 3), B // B_DEV)
    neg_owner = jax.vmap(lambda own, number: shared_out(jax.random.fold_in(streams_of[3], 2), own, number, B_DEV, N_DP, NEG, CAP, 2))(neg_owner_keys, neg_owner_turns).reshape((B, NEG))
    neg_row = touch_ends(jax.random.randint(streams_of[4], (B, NEG), 0, B_DEV), jax.random.fold_in(streams_of[4], 1), 0, B_DEV - 1).astype(jnp.int32)
    return {"queries": queries, "passages": passages, "negatives": negatives, "neg_owner": neg_owner, "neg_row": neg_row}


def reference(queries, passages, negatives, neg_owner, neg_row):
    score_scale = D ** -0.5
    pool_index = (neg_owner * B_DEV + neg_row).astype(jnp.int32)
    scores = jnp.dot(queries, passages.T, preferred_element_type=jnp.float32) * score_scale
    pool_scores = jnp.dot(queries, negatives.T, preferred_element_type=jnp.float32) * score_scale
    neg_scores = jnp.take_along_axis(pool_scores, pool_index, axis=1)
    row_peak = jnp.maximum(jnp.max(scores, axis=1), jnp.max(neg_scores, axis=1))
    row_total = jnp.sum(jnp.exp(scores - row_peak[:, None]), axis=1) + jnp.sum(jnp.exp(neg_scores - row_peak[:, None]), axis=1)
    log_total = row_peak + jnp.log(row_total)
    row_loss = log_total - jnp.diagonal(scores)
    identity = (jnp.arange(B, dtype=jnp.int32)[:, None] == jnp.arange(B, dtype=jnp.int32)[None, :]).astype(jnp.float32)
    soft_weight = (jnp.exp(scores - log_total[:, None]) - identity).astype(jnp.bfloat16)
    neg_weight = jnp.exp(neg_scores - log_total[:, None])
    query_values = queries.astype(jnp.float32)

    def add_negative(carry, inputs):
        index_column, weight_column = inputs
        picked_rows = jnp.take(negatives, index_column, axis=0).astype(jnp.float32)
        grad_inner = carry[0] + weight_column[:, None] * picked_rows
        contribution = (score_scale * weight_column[:, None] * query_values).astype(jnp.bfloat16)
        contribution = lax.optimization_barrier(contribution).astype(jnp.float32)
        grad_pool = carry[1] + jax.ops.segment_sum(contribution, index_column, num_segments=B)
        return (grad_inner, grad_pool), None

    start_carry = (jnp.zeros((B, D), jnp.float32), jnp.zeros((B, D), jnp.float32))
    (grad_inner, grad_pool), unused = lax.scan(add_negative, start_carry, (pool_index.T, neg_weight.T))
    grad_queries = (score_scale * (jnp.dot(soft_weight, passages, preferred_element_type=jnp.float32) + grad_inner)).astype(jnp.bfloat16)
    grad_passages = (score_scale * jnp.dot(soft_weight.T, queries, preferred_element_type=jnp.float32)).astype(jnp.bfloat16)
    return row_loss, grad_queries, grad_passages, grad_pool.astype(jnp.bfloat16)
```

```python
import jax
import jax.numpy as jnp
from jax import lax
from jax.sharding import Mesh, PartitionSpec as P

F32 = jnp.float32
BF16 = jnp.bfloat16


def ring(count, step):
    return [(i, (i + step) % count) for i in range(count)]


def shift(x, axis, count, step):
    return lax.ppermute(x, axis, ring(count, step))


def add(a, b):
    return (a.astype(F32) + b.astype(F32)).astype(BF16)


def gather_z(x):
    half = 48
    r1 = shift(x, "z", 8, 1)
    l1 = shift(x, "z", 8, -1)
    r2 = shift(r1, "z", 8, 1)
    l2 = shift(l1, "z", 8, -1)
    r3 = shift(r2, "z", 8, 1)
    l3 = shift(l2, "z", 8, -1)
    r4 = shift(r3[:half], "z", 8, 1)
    l4 = shift(l3[half:], "z", 8, -1)
    return [x, r1, r2, r3, jnp.concatenate([r4, l4]), l3, l2, l1]


def gather_y(x, half):
    r1 = shift(x, "y", 4, 1)
    l1 = shift(x, "y", 4, -1)
    r2 = shift(r1[:half], "y", 4, 1)
    l2 = shift(l1[half:], "y", 4, -1)
    return [x, r1, jnp.concatenate([r2, l2]), l1]


def reduce_y(parts, half):
    a = shift(parts[2][:half].astype(BF16), "y", 4, 1)
    b = shift(parts[2][half:].astype(BF16), "y", 4, -1)
    right = jnp.concatenate([add(parts[3][:half], a), parts[3][half:].astype(BF16)])
    left = jnp.concatenate([parts[1][:half].astype(BF16), add(parts[1][half:], b)])
    c = shift(right, "y", 4, 1)
    d = shift(left, "y", 4, -1)
    return parts[0].astype(F32) + c.astype(F32) + d.astype(F32)


def reduce_z(block_of):
    half = 48
    far = block_of(4)
    a = shift(far[:half].astype(BF16), "z", 8, 1)
    b = shift(far[half:].astype(BF16), "z", 8, -1)
    r = block_of(3)
    l = block_of(-3)
    r = jnp.concatenate([add(r[:half], a), r[half:].astype(BF16)])
    l = jnp.concatenate([l[:half].astype(BF16), add(l[half:], b)])
    for s in (2, 1):
        r = add(block_of(s), shift(r, "z", 8, 1))
        l = add(block_of(-s), shift(l, "z", 8, -1))
    r = shift(r, "z", 8, 1)
    l = shift(l, "z", 8, -1)
    return block_of(0).astype(F32) + r.astype(F32) + l.astype(F32)


def local(queries, passages, negatives, neg_owner, neg_row):
    rows, features = queries.shape
    neg_count = neg_owner.shape[1]
    scale = (features * 4) ** (-0.5)
    y = lax.axis_index("y")
    z = lax.axis_index("z")
    xl = lax.axis_index("xl")
    xh = lax.axis_index("xh")
    core = lax.axis_index("c")
    total = 8 * rows
    wide = 768

    names = jnp.concatenate([neg_owner, neg_row], axis=1).astype(BF16)
    names = jnp.pad(names, ((0, 0), (0, 128 - 2 * neg_count)))
    blocks = gather_z(jnp.concatenate([queries, names], axis=1))
    rel = jnp.concatenate(blocks[::-1])
    rel = jnp.concatenate([rel, rel])
    q_all = lax.dynamic_slice(rel, (((7 - z) % 8) * rows, 0), (total, rel.shape[1]))
    owner = q_all[:, features : features + neg_count].astype(jnp.int32)
    row = q_all[:, features + neg_count : features + 2 * neg_count].astype(jnp.int32)
    q_all = q_all[:, :features]

    p_pair = jnp.concatenate([passages, shift(passages, "xl", 2, 1)])
    p_all = jnp.concatenate(gather_y(p_pair, rows))
    n_line = jnp.concatenate(gather_y(negatives, 48))
    n_all = jnp.concatenate([n_line, shift(n_line, "xl", 2, 1)])

    owner_y, owner_z, owner_x = owner // 16, (owner // 2) % 8, owner % 2
    place = ((owner_x != xl).astype(jnp.int32) * 4 + (y - owner_y) % 4) * rows + row
    place = jnp.where(owner_z == z, place, -1)

    s_part = lax.dot_general(q_all, p_all, (((1,), (1,)), ((), ())), preferred_element_type=F32)
    n_part = lax.dot_general(q_all, n_all, (((1,), (1,)), ((), ())), preferred_element_type=F32)
    column = lax.broadcasted_iota(jnp.int32, (total, total), 1)
    picked = [
        jnp.sum(jnp.where(place[:, k : k + 1] == column, n_part, 0.0), axis=1, keepdims=True)
        for k in range(neg_count)
    ]
    ext = jnp.concatenate(
        [s_part] + picked + [jnp.zeros((total, wide - total - neg_count), F32)], axis=1
    )

    quarter = total // 4
    ext = ext.reshape(2, 2, quarter, wide)
    mine = lax.dynamic_index_in_dim(ext, core, 1, keepdims=False)
    other = lax.dynamic_index_in_dim(ext, 1 - core, 1, keepdims=False)
    mine = mine + shift(other, "c", 2, 1)
    keep = lax.dynamic_index_in_dim(mine, xh, 0, keepdims=False)
    give = lax.dynamic_index_in_dim(mine, 1 - xh, 0, keepdims=False)
    summed = (keep + shift(give, "xh", 2, 1)) * scale

    first = (xh * 2 + core) * quarter
    place_q = lax.dynamic_slice(place, (first, 0), (quarter, neg_count))
    scores = summed[:, :total]
    neg_scores = jnp.where(place_q >= 0, summed[:, total : total + neg_count], -jnp.inf)
    peak = jnp.maximum(jnp.max(scores, axis=1), jnp.max(neg_scores, axis=1))
    part_sum = jnp.sum(jnp.exp(scores - peak[:, None]), axis=1) + jnp.sum(
        jnp.exp(neg_scores - peak[:, None]), axis=1
    )
    row_id = first + lax.broadcasted_iota(jnp.int32, (quarter, total), 0)
    place_id = lax.broadcasted_iota(jnp.int32, (quarter, total), 1)
    hits = jnp.logical_and(row_id - z * rows == place_id, place_id < rows)
    positive = jnp.sum(jnp.where(hits, scores, 0.0), axis=1)
    stats = jnp.stack([peak, part_sum, positive])
    every = jnp.stack([stats] + [shift(stats, "z", 8, s) for s in range(1, 8)])
    all_peak = jnp.max(every[:, 0], axis=0)
    all_sum = jnp.sum(every[:, 1] * jnp.exp(every[:, 0] - all_peak), axis=0)
    log_total = all_peak + jnp.log(all_sum)
    loss = log_total - jnp.sum(every[:, 2], axis=0)

    soft = jnp.exp(scores - log_total[:, None]) - hits.astype(F32)
    neg_w = jnp.exp(neg_scores - log_total[:, None])
    neg_hi = neg_w.astype(BF16)
    neg_lo = (neg_w - neg_hi.astype(F32)).astype(BF16)
    loss_hi = loss.astype(BF16)
    rest = loss - loss_hi.astype(F32)
    loss_mid = rest.astype(BF16)
    loss_lo = (rest - loss_mid.astype(F32)).astype(BF16)
    ext = jnp.concatenate(
        [soft.astype(BF16), neg_hi, neg_lo]
        + [v[:, None] for v in (loss_hi, loss_mid, loss_lo)]
        + [jnp.zeros((quarter, wide - total - 2 * neg_count - 3), BF16)],
        axis=1,
    )
    ext = lax.all_gather(ext, ("xh", "c"), axis=0, tiled=True)
    weight = ext[:, :total]
    tail = ext[:, total:].astype(F32)
    neg_hi = tail[:, :neg_count]
    neg_lo = tail[:, neg_count : 2 * neg_count]
    loss = jnp.sum(tail[:, 2 * neg_count : 2 * neg_count + 3], axis=1)
    row_loss = lax.dynamic_slice(loss, (z * rows,), (rows,))

    neg_weight = jnp.zeros((total, total), F32)
    neg_rest = jnp.zeros((total, total), F32)
    for k in range(neg_count):
        hit = place[:, k : k + 1] == column
        neg_weight = jnp.where(hit, neg_hi[:, k : k + 1], neg_weight)
        neg_rest = jnp.where(hit, neg_lo[:, k : k + 1], neg_rest)
    neg_weight = neg_weight.astype(BF16)
    neg_rest = neg_rest.astype(BF16)

    def rows_by(a, b):
        return lax.dot_general(a, b, (((1,), (0,)), ((), ())), preferred_element_type=F32)

    def cols_by(a, b):
        return lax.dot_general(a, b, (((0,), (0,)), ((), ())), preferred_element_type=F32)

    gq = scale * (rows_by(weight, p_all) + rows_by(neg_weight, n_all) + rows_by(neg_rest, n_all))
    gp = scale * cols_by(weight, q_all)
    gn = scale * (cols_by(neg_weight, q_all) + cols_by(neg_rest, q_all))

    grad_queries = reduce_z(
        lambda s: lax.dynamic_slice(gq, (((z + s) % 8) * rows, 0), (rows, features))
    )
    pair = 2 * rows
    gp_pair = reduce_y([gp[k * pair : (k + 1) * pair] for k in range(4)], rows)
    grad_passages = gp_pair[:rows] + shift(gp_pair[rows:].astype(BF16), "xl", 2, 1).astype(F32)
    line = 4 * rows
    gn_line = gn[:line] + shift(gn[line:].astype(BF16), "xl", 2, 1).astype(F32)
    grad_negatives = reduce_y([gn_line[k * rows : (k + 1) * rows] for k in range(4)], 48)
    return (
        row_loss,
        grad_queries.astype(BF16),
        grad_passages.astype(BF16),
        grad_negatives.astype(BF16),
    )


def solution(mesh):
    fine = Mesh(mesh.devices.reshape(4, 8, 2, 2, 2), ("y", "z", "xl", "xh", "c"))
    dp, width = ("y", "z", "xl"), ("xh", "c")
    in_specs = (P(dp, width), P(dp, width), P(dp, width), P(dp, None), P(dp, None))
    out_specs = (P(dp), P(dp, width), P(dp, width), P(dp, width))
    return jax.shard_map(local, mesh=fine, in_specs=in_specs, out_specs=out_specs, check_vma=False)
```

```python
import functools

import jax
import jax.numpy as jnp
from jax import lax
from jax.experimental import pallas as pl
from jax.experimental.pallas import tpu as pltpu
from jax.sharding import Mesh, PartitionSpec as P

F32 = jnp.float32
BF16 = jnp.bfloat16
NEG = 7
ROWS = 88
FEAT = 1024
TOTAL = 8 * ROWS
QUARTER = 2 * ROWS
WIDE = 768
SCALE = 4096 ** (-0.5)
VMEM_LIMIT = 48 * 1024 * 1024
NT = (((1,), (1,)), ((), ()))
NN = (((1,), (0,)), ((), ()))
TN = (((0,), (0,)), ((), ()))


def shift(x, axis, count, step):
    return lax.ppermute(x, axis, [(i, (i + step) % count) for i in range(count)])


def add(a, b):
    return (a.astype(F32) + b.astype(F32)).astype(BF16)


def gather_z(x):
    half = 48
    r1 = shift(x, "z", 8, 1)
    l1 = shift(x, "z", 8, -1)
    r2 = shift(r1, "z", 8, 1)
    l2 = shift(l1, "z", 8, -1)
    r3 = shift(r2, "z", 8, 1)
    l3 = shift(l2, "z", 8, -1)
    r4 = shift(r3[:half], "z", 8, 1)
    l4 = shift(l3[half:], "z", 8, -1)
    return jnp.concatenate([x, r1, r2, r3, r4, l4, l3, l2, l1])


def reduce_z(partial):
    def block(s):
        k = (-s) % 8
        return partial[k * ROWS : (k + 1) * ROWS]

    half = 48
    far = block(4).astype(BF16)
    a = shift(far[:half], "z", 8, 1)
    b = shift(far[half:], "z", 8, -1)
    r, l = block(3), block(-3)
    r = jnp.concatenate([add(r[:half], a), r[half:].astype(BF16)])
    l = jnp.concatenate([l[:half].astype(BF16), add(l[half:], b)])
    for s in (2, 1):
        r = add(block(s), shift(r, "z", 8, 1))
        l = add(block(-s), shift(l, "z", 8, -1))
    r = shift(r, "z", 8, 1)
    l = shift(l, "z", 8, -1)
    return block(0).astype(F32) + r.astype(F32) + l.astype(F32)


def places(names, at):
    names = names.astype(F32).astype(jnp.int32)
    owner, row = names[:, :NEG], names[:, NEG : 2 * NEG]
    owner_y, owner_z, owner_x = owner >> 4, (owner >> 1) & 7, owner & 1
    place = (jnp.where(owner_x != at[2], 4, 0) + owner_y) * ROWS + row
    return jnp.where(owner_z == at[1], place, -1)


def pack_kernel(q_ref, owner_ref, row_ref, out_ref):
    out_ref[:, :FEAT] = q_ref[...]
    out_ref[:, FEAT:] = jnp.zeros((ROWS, 128), BF16)
    out_ref[:, FEAT : FEAT + NEG] = owner_ref[...].astype(F32).astype(BF16)
    out_ref[:, FEAT + NEG : FEAT + 2 * NEG] = row_ref[...].astype(F32).astype(BF16)


def score_kernel(at_ref, q_ref, names_ref, p_ref, n0_ref, n1_ref, out_ref):
    q = q_ref[...]
    out_ref[0, :, :TOTAL] = lax.dot_general(q, p_ref[...], NT, preferred_element_type=F32)
    place = places(names_ref[...], (at_ref[0], at_ref[1], at_ref[2]))
    near = lax.dot_general(q, n0_ref[...], NT, preferred_element_type=F32)
    far = lax.dot_general(q, n1_ref[...], NT, preferred_element_type=F32)
    column = lax.broadcasted_iota(jnp.int32, near.shape, 1)
    lane = lax.broadcasted_iota(jnp.int32, (QUARTER, WIDE - TOTAL), 1)
    tail = jnp.full((QUARTER, WIDE - TOTAL), -jnp.inf, F32)
    for k in range(NEG):
        at_k = place[:, k : k + 1]
        value = jnp.sum(
            jnp.where(at_k == column, near, 0.0)
            + jnp.where(at_k - near.shape[1] == column, far, 0.0),
            axis=1,
            keepdims=True,
        )
        value = jnp.where(at_k >= 0, value, -jnp.inf)
        tail = jnp.where((lane == k) | (lane == k + NEG), value, tail)
    out_ref[0, :, TOTAL:] = tail


def soft_kernel(at_ref, keep_ref, near_ref, far_ref, e_ref, stats_ref, turn_ref):
    scores = (keep_ref[0] + near_ref[0] + far_ref[0]) * SCALE
    peak = jnp.max(scores, axis=1, keepdims=True)
    e = jnp.exp(scores - peak)
    column = lax.broadcasted_iota(jnp.int32, scores.shape, 1)
    once = column < TOTAL + NEG
    part = jnp.sum(jnp.where(once, e, 0.0), axis=1, keepdims=True)
    e_high = e.astype(BF16)
    e_ref[...] = jnp.where(once, e_high.astype(F32), e - e_high.astype(F32)).astype(BF16)
    row = lax.broadcasted_iota(jnp.int32, scores.shape, 0)
    own = (column == row + at_ref[0] * QUARTER) & (row < ROWS)
    positive = jnp.sum(jnp.where(own, scores, 0.0), axis=1, keepdims=True)
    lane = lax.broadcasted_iota(jnp.int32, (QUARTER, 128), 1)
    info = jnp.where(lane == 0, peak, jnp.where(lane == 1, part, positive))
    stats_ref[...] = jnp.zeros((8, 128), F32)
    for h in range(2):
        turn_ref[...] = jnp.zeros((128, 128), F32)
        turn_ref[:ROWS, :] = info[h * ROWS : (h + 1) * ROWS]
        turned = jnp.transpose(turn_ref[...])
        for v in range(3):
            stats_ref[2 * v + h : 2 * v + h + 1, :] = turned[v : v + 1, :]


def weight_kernel(
    at_ref, stats_ref, e0_ref, e1_ref, e2_ref, e3_ref, names_ref,
    w_ref, high_ref, low_ref, loss_ref, peak_ref, part_ref, turn_ref,
):
    y, z, xl = at_ref[0], at_ref[1], at_ref[2]
    xh, core = at_ref[3], at_ref[4]
    for d in range(8):
        source = lax.rem(z + d, 8)
        for k in range(8):
            j = (k + d) % 8
            quarter, h = j // 2, j % 2
            c_from, x_from = quarter // 2, quarter % 2
            slot = source * 4 + (x_from * 2 + c_from)
            peak_ref[d, k : k + 1, :] = stats_ref[slot, h : h + 1, :]
            part_ref[d, k : k + 1, :] = stats_ref[slot, 2 + h : 3 + h, :]
    peaks = peak_ref[...]
    top = jnp.max(peaks, axis=0)
    whole = jnp.sum(part_ref[...] * jnp.exp(peaks - top[None]), axis=0)
    log_total = top + jnp.log(whole)
    positive = stats_ref[z * 4, 4:5, :]
    loss = log_total[0:1] - positive
    loss_ref[...] = jnp.broadcast_to(loss, (8, 128))
    turn_ref[...] = jnp.zeros((128, 128), F32)
    turn_ref[0:8, :] = jnp.exp(peaks[0] - log_total)
    turn_ref[8:9, :] = jnp.exp(-loss) - 1.0
    turned = jnp.transpose(turn_ref[...])
    column = lax.broadcasted_iota(jnp.int32, (ROWS, TOTAL), 1)
    row = lax.broadcasted_iota(jnp.int32, (ROWS, TOTAL), 0)
    diagonal = column == row + y * QUARTER
    column2 = lax.broadcasted_iota(jnp.int32, (QUARTER, TOTAL), 1)
    pieces = ((e0_ref, 0, 0), (e1_ref, 1, 0), (e2_ref, 0, 1), (e3_ref, 1, 1))
    for e_ref, a, b in pieces:
        for quarter in range(4):
            c_of, x_of = quarter // 2, quarter % 2

            @pl.when((core == (c_of ^ a)) & (xh == (x_of ^ b)))
            def _(e_ref=e_ref, quarter=quarter):
                e = e_ref[...].astype(F32)
                factor = jnp.concatenate(
                    [turned[:ROWS, 2 * quarter + h : 2 * quarter + h + 1] for h in range(2)]
                )
                soft = e[:, :TOTAL] * factor
                if quarter == 0:
                    first = jnp.where(diagonal, turned[:ROWS, 8:9], soft[:ROWS])
                    soft = jnp.concatenate([first, soft[ROWS:]])
                first = quarter * QUARTER
                w_ref[first : first + QUARTER, :] = soft.astype(BF16)
                tail = (e[:, TOTAL : TOTAL + NEG] + e[:, TOTAL + NEG : TOTAL + 2 * NEG]) * factor
                place = places(names_ref[first : first + QUARTER, :], (y, z, xl))
                value = jnp.zeros((QUARTER, TOTAL), F32)
                for k in range(NEG):
                    value = jnp.where(place[:, k : k + 1] == column2, tail[:, k : k + 1], value)
                high = value.astype(BF16)
                high_ref[first : first + QUARTER, :] = high
                low_ref[first : first + QUARTER, :] = (value - high.astype(F32)).astype(BF16)


def params():
    return pltpu.CompilerParams(vmem_limit_bytes=VMEM_LIMIT)


def vmem():
    return pl.BlockSpec(memory_space=pltpu.VMEM)


def smem():
    return pl.BlockSpec(memory_space=pltpu.SMEM)


def scores_half(at, q_cat, p_all, n0, n1, give):
    def quarter(i, at):
        half = 1 - at[4] if give else at[4]
        return half * 2 + jnp.where(at[3] == i, 0, 1)

    whole = lambda i, at: (0, 0)
    return pl.pallas_call(
        score_kernel,
        out_shape=jax.ShapeDtypeStruct((2, QUARTER, WIDE), F32),
        grid_spec=pltpu.PrefetchScalarGridSpec(
            num_scalar_prefetch=1,
            grid=(2,),
            in_specs=[
                pl.BlockSpec((QUARTER, FEAT), lambda i, at: (quarter(i, at), 0)),
                pl.BlockSpec((QUARTER, 128), lambda i, at: (quarter(i, at), FEAT // 128)),
                pl.BlockSpec((TOTAL, FEAT), whole),
                pl.BlockSpec((TOTAL // 2, FEAT), whole),
                pl.BlockSpec((TOTAL // 2, FEAT), whole),
            ],
            out_specs=pl.BlockSpec((1, QUARTER, WIDE), lambda i, at: (i, 0, 0)),
        ),
        compiler_params=params(),
        cost_estimate=pl.CostEstimate(
            flops=4 * QUARTER * 2 * TOTAL * FEAT, bytes_accessed=5_000_000, transcendentals=0
        ),
        name="scores_give" if give else "scores_keep",
    )(at, q_cat, q_cat, p_all, n0, n1)


def local(queries, passages, negatives, neg_owner, neg_row):
    axes = ("y", "z", "xl", "xh", "c")
    at = jnp.stack([lax.axis_index(a) for a in axes]).astype(jnp.int32)

    packed = pl.pallas_call(
        pack_kernel,
        out_shape=jax.ShapeDtypeStruct((ROWS, FEAT + 128), BF16),
        in_specs=[vmem()] * 3,
        out_specs=vmem(),
        name="pack",
    )(queries, neg_owner, neg_row)
    q_cat = gather_z(packed)

    def everywhere_y(x):
        rows = x.shape[0]
        spread = jnp.broadcast_to(x[None], (4,) + x.shape).reshape(4 * rows, FEAT)
        return lax.all_to_all(spread, "y", 0, 0, tiled=True)

    n0 = everywhere_y(negatives)
    p_all = everywhere_y(jnp.concatenate([passages, shift(passages, "xl", 2, 1)]))
    n1 = shift(n0, "xl", 2, 1)

    give = scores_half(at, q_cat, p_all, n0, n1, True)
    near = shift(give, "c", 2, 1)
    keep = scores_half(at, q_cat, p_all, n0, n1, False)
    far = shift(keep[1:] + near[1:], "xh", 2, 1)

    one = lambda *tail: pl.BlockSpec((1,) + tail, lambda i, at: (0,) * (1 + len(tail)))
    e0, stats = pl.pallas_call(
        soft_kernel,
        out_shape=(
            jax.ShapeDtypeStruct((QUARTER, WIDE), BF16),
            jax.ShapeDtypeStruct((8, 128), F32),
        ),
        grid_spec=pltpu.PrefetchScalarGridSpec(
            num_scalar_prefetch=1,
            grid=(1,),
            in_specs=[one(QUARTER, WIDE)] * 3,
            out_specs=(
                pl.BlockSpec((QUARTER, WIDE), lambda i, at: (0, 0)),
                pl.BlockSpec((8, 128), lambda i, at: (0, 0)),
            ),
            scratch_shapes=[pltpu.VMEM((128, 128), F32)],
        ),
        compiler_params=params(),
        name="soft",
    )(at, keep, near, far)

    stats = lax.all_to_all(
        jnp.broadcast_to(stats[None], (32, 8, 128)), ("z", "xh", "c"), 0, 0, tiled=True
    )
    e2 = shift(e0, "xh", 2, 1)
    e1 = shift(e0, "c", 2, 1)
    e3 = shift(e2, "c", 2, 1)

    weight, neg_high, neg_low, loss = pl.pallas_call(
        weight_kernel,
        out_shape=(
            jax.ShapeDtypeStruct((TOTAL, TOTAL), BF16),
            jax.ShapeDtypeStruct((TOTAL, TOTAL), BF16),
            jax.ShapeDtypeStruct((TOTAL, TOTAL), BF16),
            jax.ShapeDtypeStruct((8, 128), F32),
        ),
        in_specs=[smem()] + [vmem()] * 6,
        out_specs=(vmem(),) * 4,
        scratch_shapes=[
            pltpu.VMEM((8, 8, 128), F32),
            pltpu.VMEM((8, 8, 128), F32),
            pltpu.VMEM((128, 128), F32),
        ],
        compiler_params=params(),
        name="weights",
    )(at, stats, e0, e1, e2, e3, q_cat[:, FEAT:])

    def dot(a, b, dims):
        return lax.dot_general(a, b, dims, preferred_element_type=F32)

    q_all = q_cat[:, :FEAT]
    n_all = jnp.concatenate([n0, n1])
    gq = SCALE * (dot(weight, p_all, NN) + dot(neg_high, n_all, NN))
    gp = (SCALE * dot(weight, q_all, TN)).astype(BF16)
    gn = SCALE * (dot(neg_high, q_all, TN) + dot(neg_low, q_all, TN))

    grad_queries = reduce_z(gq)
    gp = lax.all_to_all(gp, "y", 0, 0, tiled=True).reshape(4, 2 * ROWS, FEAT)
    gp = jnp.sum(gp.astype(F32), axis=0)
    grad_passages = gp[:ROWS] + shift(gp[ROWS:].astype(BF16), "xl", 2, 1).astype(F32)
    line = 4 * ROWS
    gn = add(gn[:line], shift(gn[line:].astype(BF16), "xl", 2, 1))
    gn = lax.all_to_all(gn, "y", 0, 0, tiled=True).reshape(4, ROWS, FEAT)
    grad_negatives = jnp.sum(gn.astype(F32), axis=0)
    return (
        loss[0, :ROWS],
        grad_queries.astype(BF16),
        grad_passages.astype(BF16),
        grad_negatives.astype(BF16),
    )


def solution(mesh):
    fine = Mesh(mesh.devices.reshape(4, 8, 2, 2, 2), ("y", "z", "xl", "xh", "c"))
    dp, width = ("y", "z", "xl"), ("xh", "c")
    in_specs = (P(dp, width), P(dp, width), P(dp, width), P(dp, None), P(dp, None))
    out_specs = (P(dp), P(dp, width), P(dp, width), P(dp, width))
    return jax.shard_map(local, mesh=fine, in_specs=in_specs, out_specs=out_specs, check_vma=False)
```

```python
import functools

import jax
import jax.numpy as jnp
from jax import lax
from jax.experimental import pallas as pl
from jax.experimental.pallas import tpu as pltpu
from jax.sharding import Mesh, PartitionSpec as P

F32 = jnp.float32
BF16 = jnp.bfloat16
NEG = 7
ROWS = 88
FEAT = 1024
TOTAL = 8 * ROWS
QUARTER = 2 * ROWS
WIDE = 768
SCALE = 4096 ** (-0.5)
VMEM_LIMIT = 20 * 1024 * 1024
LAST = 640
NT = (((1,), (1,)), ((), ()))
NN = (((1,), (0,)), ((), ()))
TN = (((0,), (0,)), ((), ()))


def shift(x, axis, count, step):
    return lax.ppermute(x, axis, [(i, (i + step) % count) for i in range(count)])


def gather_z(x):
    half = 48
    r1 = shift(x, "z", 8, 1)
    l1 = shift(x, "z", 8, -1)
    r2 = shift(r1, "z", 8, 1)
    l2 = shift(l1, "z", 8, -1)
    r3 = shift(r2, "z", 8, 1)
    l3 = shift(l2, "z", 8, -1)
    r4 = shift(r3[:half], "z", 8, 1)
    l4 = shift(l3[half:], "z", 8, -1)
    return jnp.concatenate([x, r1, r2, r3, r4, l4, l3, l2, l1])


def prepare_kernel(q_ref, p_ref, n_ref, owner_ref, row_ref, q_out_ref, out_ref, turn_ref):
    q_out_ref[:, :FEAT] = q_ref[...]
    lane = lax.broadcasted_iota(jnp.int32, (ROWS, 128), 1)
    lane = lane.astype(F32)
    turn_ref[...] = jnp.zeros((128, 128), F32)
    turn_ref[:NEG, :ROWS] = owner_ref[...].astype(F32)
    turn_ref[8 : 8 + NEG, :ROWS] = row_ref[...].astype(F32)
    turned = jnp.transpose(turn_ref[...])[:ROWS]
    named = jnp.full((ROWS, 128), -1.0, F32)
    for k in range(NEG):
        named = jnp.where(lane == turned[:, k : k + 1], turned[:, 8 + k : 9 + k], named)
    q_out_ref[:, FEAT:] = named.astype(BF16)
    for b in range(8):
        out_ref[b, :, :FEAT] = p_ref[...]
        out_ref[b, :, FEAT:] = n_ref[...]


def position(*axes):
    return tuple(lax.axis_index(a) for a in axes)


def in_block(column, b):
    return (column >= b * ROWS) & (column < b * ROWS + ROWS)


def named_mask(names, z):
    owner = lax.broadcasted_iota(jnp.int32, (128, TOTAL), 0)
    column = lax.broadcasted_iota(jnp.int32, (128, TOTAL), 1)
    here = (owner < 64) & (((owner >> 1) & 7) == z)
    spot = (owner >> 4) * 2 + (owner & 1)
    spread = jnp.where(here & in_block(column, spot), 1.0, 0.0).astype(BF16)
    wanted = lax.dot_general(names, spread, NN, preferred_element_type=F32)
    inner = column[:8]
    for b in range(1, 8):
        inner = inner - jnp.where(column[:8] >= b * ROWS, ROWS, 0)
    return wanted == inner[:1].astype(F32), here, spot


def score_kernel(give, q_ref, pn_ref, out_ref):
    z, xh, core = position("z", "xh", "c")
    half = 1 - core if give else core
    mine = pl.ds(pl.multiple_of(half * 2 * QUARTER, 2 * QUARTER), 2 * QUARTER)
    names = q_ref[mine, FEAT:]
    mask, here, spot = named_mask(names, z)
    q = q_ref[mine, :FEAT]
    named = lax.dot_general(q, pn_ref[:, FEAT:], NT, preferred_element_type=F32)
    row = lax.broadcasted_iota(jnp.int32, (TOTAL, 128), 0)
    lane = lax.broadcasted_iota(jnp.int32, (TOTAL, 128), 1)
    gather = jnp.where((lane < 16) & in_block(row, lane & 7), 1.0, 0.0)
    value = lax.dot_general(
        jnp.where(mask, named, 0.0), gather, NN,
        precision=lax.Precision.HIGHEST, preferred_element_type=F32,
    )
    lane_b = lax.broadcasted_iota(jnp.int32, (128, 128), 1)
    pick = here[:, :128] & (spot[:, :128] == (lane_b & 7)) & (lane_b < 16)
    at_block = lax.dot_general(
        names, jnp.where(pick, 1.0, 0.0).astype(BF16), NN, preferred_element_type=F32
    )
    tail = jnp.where((at_block >= 0.0) & (lane[: 2 * QUARTER] < 16), value, -jnp.inf)
    scores = lax.dot_general(q, pn_ref[:, :FEAT], NT, preferred_element_type=F32)
    for j in range(2):
        slot = pl.ds(jnp.where(xh == j, 0, 1), 1)
        rows = slice(j * QUARTER, (j + 1) * QUARTER)
        out_ref[slot, :, :TOTAL] = scores[None, rows]
        out_ref[slot, :, TOTAL:] = tail[None, rows, : WIDE - TOTAL]


def soft_kernel(keep_ref, near_ref, far_ref, e_ref, stats_out_ref, turn_ref, stats_ref, sem):
    y, xl = position("y", "xl")
    scores = (keep_ref[0] + near_ref[0] + far_ref[0]) * SCALE
    peak = jnp.max(scores, axis=1, keepdims=True)
    e = jnp.exp(scores - peak)
    column = lax.broadcasted_iota(jnp.int32, scores.shape, 1)
    once = column < TOTAL + 8
    part = jnp.sum(jnp.where(once, e, 0.0), axis=1, keepdims=True)
    lane = lax.broadcasted_iota(jnp.int32, (QUARTER, 128), 1)
    column = lax.broadcasted_iota(jnp.int32, scores.shape, 1)
    row = lax.broadcasted_iota(jnp.int32, scores.shape, 0)
    own = (column == row + (y * 2 + xl) * ROWS) & (row < ROWS)
    positive = jnp.sum(jnp.where(own, scores, 0.0), axis=1, keepdims=True)
    info = jnp.where(lane == 0, peak, jnp.where(lane == 1, part, positive))
    stats_ref[...] = jnp.zeros(stats_ref.shape, F32)
    for h in range(2):
        turn_ref[...] = jnp.zeros((128, 128), F32)
        turn_ref[:ROWS, :] = info[h * ROWS : (h + 1) * ROWS]
        turned = jnp.transpose(turn_ref[...])
        for v in range(3):
            at = 2 * v + h
            stats_ref[:, at : at + 1, :] = jnp.broadcast_to(turned[None, v : v + 1], (32, 1, 128))
    copy = pltpu.make_async_copy(stats_ref, stats_out_ref, sem)
    copy.start()
    high = e.astype(BF16).astype(F32)
    e_ref[...] = jnp.where(once, high, e - high).astype(BF16)
    copy.wait()


PIECES = ((0, 0), (1, 0), (0, 1), (1, 1))


def per_quarter(xh, core, refs, body):
    for ref, (a, b) in zip(refs, PIECES):
        for quarter in range(4):
            c_of, x_of = quarter // 2, quarter % 2
            pl.when((core == (c_of ^ a)) & (xh == (x_of ^ b)))(functools.partial(body, ref, quarter))


def weight_kernel(
    stats_ref, e0_ref, e1_ref, e2_ref, e3_ref, pn_ref, q_far_ref,
    out_far_ref, gq_out_ref, loss_ref,
    out_ref, w_ref, high_ref, low_ref, gq_ref, mask_ref, q_ref,
    peak_ref, part_ref, turn_ref, sem,
):
    y, z, xl, xh, core = position("y", "z", "xl", "xh", "c")
    load = pltpu.make_async_copy(q_far_ref, q_ref, sem.at[0])
    load.start()
    for d in range(8):
        source = lax.rem(z + d, 8)
        for k in range(8):
            j = (k + d) % 8
            quarter, h = j // 2, j % 2
            c_from, x_from = quarter // 2, quarter % 2
            slot = source * 4 + (x_from * 2 + c_from)
            peak_ref[d, k : k + 1, :] = stats_ref[slot, h : h + 1, :]
            part_ref[d, k : k + 1, :] = stats_ref[slot, 2 + h : 3 + h, :]
    peaks = peak_ref[...]
    top = jnp.max(peaks, axis=0)
    whole = jnp.sum(part_ref[...] * jnp.exp(peaks - top[None]), axis=0)
    log_total = top + jnp.log(whole)
    positive = stats_ref[z * 4, 4:5, :]
    loss = log_total[0:1] - positive
    loss_ref[...] = jnp.broadcast_to(loss, (8, 128))
    turn_ref[...] = jnp.zeros((128, 128), F32)
    turn_ref[0:8, :] = jnp.exp(peaks[0] - log_total)
    turn_ref[8:9, :] = jnp.exp(-loss) - 1.0
    turned = jnp.transpose(turn_ref[...])
    column = lax.broadcasted_iota(jnp.int32, (ROWS, TOTAL), 1)
    row = lax.broadcasted_iota(jnp.int32, (ROWS, TOTAL), 0)
    diagonal = column == row + (y * 2 + xl) * ROWS

    lane = lax.broadcasted_iota(jnp.int32, (128, TOTAL), 0) - (TOTAL - LAST)
    wide = lax.broadcasted_iota(jnp.int32, (128, TOTAL), 1)
    spread = (lane >= 0) & (lane < 16) & in_block(wide, lane & 7)
    spread = jnp.where(spread, 1.0, 0.0).astype(BF16)

    def body(e_ref, quarter):
        rows = slice(quarter * QUARTER, (quarter + 1) * QUARTER)
        e = e_ref[:, :TOTAL].astype(F32)
        value = lax.dot_general(e_ref[:, LAST:], spread, NN, preferred_element_type=F32)
        value = value * mask_ref[rows, :].astype(F32)
        soft, named = [], []
        for h in range(2):
            k = 2 * quarter + h
            factor = turned[:ROWS, k : k + 1]
            part = e[h * ROWS : (h + 1) * ROWS] * factor
            if k == 0:
                part = jnp.where(diagonal, turned[:ROWS, 8:9], part)
            soft.append(part)
            named.append(value[h * ROWS : (h + 1) * ROWS] * factor)
        w_ref[rows, :] = jnp.concatenate(soft).astype(BF16)
        value = jnp.concatenate(named)
        high = value.astype(BF16)
        high_ref[rows, :] = high
        low_ref[rows, :] = (value - high.astype(F32)).astype(BF16)

    load.wait()
    mask_ref[...] = jnp.where(named_mask(q_ref[:, FEAT:], z)[0], 1.0, 0.0).astype(BF16)
    pieces = ((e0_ref, 0, 0), (e1_ref, 1, 0), (e2_ref, 0, 1), (e3_ref, 1, 1))
    for e_ref, a, b in pieces:
        for quarter in range(4):
            c_of, x_of = quarter // 2, quarter % 2
            here = (core == (c_of ^ a)) & (xh == (x_of ^ b))
            pl.when(here)(functools.partial(body, e_ref, quarter))

    def dot(a, b, dims):
        return lax.dot_general(a, b, dims, preferred_element_type=F32)

    gq = dot(w_ref[...], pn_ref[:, :FEAT], NN) + dot(high_ref[...], pn_ref[:, FEAT:], NN)
    gq = SCALE * gq
    for k in range(8):
        gq_ref[pl.ds(lax.rem(z - k + 8, 8), 1)] = gq[None, k * ROWS : (k + 1) * ROWS]
    copy = pltpu.make_async_copy(gq_ref, gq_out_ref, sem.at[1])
    copy.start()
    q = q_ref[:, :FEAT]
    out_ref[:, :FEAT] = (SCALE * dot(w_ref[...], q, TN)).astype(BF16)
    front = pltpu.make_async_copy(out_ref.at[:, :FEAT], out_far_ref.at[:, :FEAT], sem.at[2])
    front.start()
    gn = dot(high_ref[...], q, TN) + dot(low_ref[...], q, TN)
    out_ref[:, FEAT:] = (SCALE * gn).astype(BF16)
    back = pltpu.make_async_copy(out_ref.at[:, FEAT:], out_far_ref.at[:, FEAT:], sem.at[3])
    back.start()
    copy.wait()
    front.wait()
    back.wait()


def finish_kernel(gq_ref, x_ref, gq_out_ref, gp_out_ref, gn_out_ref):
    gq_out_ref[...] = gq_ref[...].astype(BF16)
    for first, out_ref in ((0, gp_out_ref), (FEAT, gn_out_ref)):
        total = x_ref[0, :, first : first + FEAT].astype(F32)
        for b in range(1, 8):
            total += x_ref[b, :, first : first + FEAT].astype(F32)
        out_ref[...] = total.astype(BF16)


def call(kernel, name, operands, outs, scratch=(), far_in=0, far_out=(), limit=20):
    vmem = pl.BlockSpec(memory_space=pltpu.VMEM)
    hbm = pl.BlockSpec(memory_space=pltpu.HBM)
    return pl.pallas_call(
        kernel,
        out_shape=outs,
        in_specs=[vmem] * (len(operands) - far_in) + [hbm] * far_in,
        out_specs=tuple(hbm if i in far_out else vmem for i in range(len(outs))),
        scratch_shapes=scratch,
        compiler_params=pltpu.CompilerParams(vmem_limit_bytes=limit * 1024 * 1024),
        cost_estimate=pl.CostEstimate(flops=0, bytes_accessed=1024, transcendentals=0),
        name=name,
    )(*operands)


def shaped(shape, dtype):
    return jax.ShapeDtypeStruct(shape, dtype)


def local(queries, passages, negatives, neg_owner, neg_row):
    plane = ("y", "xl")

    packed, spread = pl.pallas_call(
        prepare_kernel,
        out_shape=(shaped((ROWS, FEAT + 128), BF16), shaped((8, ROWS, 2 * FEAT), BF16)),
        compiler_params=pltpu.CompilerParams(vmem_limit_bytes=60 * 1024 * 1024),
        grid=(1,),
        in_specs=[pl.BlockSpec((ROWS, FEAT), lambda i: (0, 0))] * 3
        + [pl.BlockSpec((NEG, ROWS), lambda i: (0, 0))] * 2,
        out_specs=(
            pl.BlockSpec((ROWS, FEAT + 128), lambda i: (0, 0)),
            pl.BlockSpec((8, ROWS, 2 * FEAT), lambda i: (0, 0, 0)),
        ),
        scratch_shapes=[pltpu.VMEM((128, 128), F32)],
        name="prepare",
    )(queries, passages, negatives, neg_owner.T, neg_row.T)
    pn = lax.all_to_all(spread, plane, 0, 0, tiled=True).reshape(TOTAL, 2 * FEAT)
    q_cat = gather_z(packed)

    def scores_half(give):
        return call(
            functools.partial(score_kernel, give), "scores_give" if give else "scores_keep",
            (q_cat, pn), (shaped((2, QUARTER, WIDE), F32),),
        )[0]

    give = scores_half(True)
    near = shift(give, "c", 2, 1)
    keep = scores_half(False)
    far = shift(keep[1:] + near[1:], "xh", 2, 1)

    e0, stats = call(
        soft_kernel, "soft", (keep, near, far),
        (shaped((QUARTER, WIDE), BF16), shaped((32, 8, 128), F32)),
        [pltpu.VMEM((128, 128), F32), pltpu.VMEM((32, 8, 128), F32), pltpu.SemaphoreType.DMA],
        far_out=(1,),
    )
    stats = lax.all_to_all(stats, ("z", "xh", "c"), 0, 0, tiled=True)
    e2 = shift(e0, "xh", 2, 1)
    e1 = shift(e0, "c", 2, 1)
    e2, stats = lax.optimization_barrier((e2, stats))
    e3 = shift(e2, "c", 2, 1)

    gpn, gq, loss = call(
        weight_kernel, "weights",
        (stats, e0, e1, e2, e3, pn, q_cat),
        (
            shaped((TOTAL, 2 * FEAT), BF16), shaped((8, ROWS, FEAT), F32), shaped((8, 128), F32),
        ),
        [pltpu.VMEM((TOTAL, 2 * FEAT), BF16)]
        + [pltpu.VMEM((TOTAL, TOTAL), BF16)] * 3
        + [pltpu.VMEM((8, ROWS, FEAT), F32)]
        + [pltpu.VMEM((TOTAL, TOTAL), BF16), pltpu.VMEM((TOTAL, FEAT + 128), BF16)]
        + [pltpu.VMEM((8, 8, 128), F32)] * 2
        + [pltpu.VMEM((128, 128), F32), pltpu.SemaphoreType.DMA((4,))],
        far_in=1,
        far_out=(0, 1),
        limit=58,
    )
    grad_queries = lax.psum_scatter(gq, "z", scatter_dimension=0, tiled=True)[0]
    gpn = lax.all_to_all(gpn.reshape(8, ROWS, 2 * FEAT), plane, 0, 0, tiled=True)

    vmem = pl.BlockSpec(memory_space=pltpu.VMEM)
    grads = pl.pallas_call(
        finish_kernel,
        out_shape=(shaped((ROWS, FEAT), BF16),) * 3,
        grid=(1,),
        in_specs=[vmem, vmem],
        out_specs=(pl.BlockSpec((ROWS, FEAT), lambda i: (0, 0)),) * 3,
        compiler_params=pltpu.CompilerParams(vmem_limit_bytes=VMEM_LIMIT),
        name="finish",
    )(grad_queries, gpn)
    return (loss[0, :ROWS],) + tuple(grads)


def solution(mesh):
    fine = Mesh(mesh.devices.reshape(4, 8, 2, 2, 2), ("y", "z", "xl", "xh", "c"))
    dp, width = ("y", "z", "xl"), ("xh", "c")
    in_specs = (P(dp, width), P(dp, width), P(dp, width), P(dp, None), P(dp, None))
    out_specs = (P(dp), P(dp, width), P(dp, width), P(dp, width))
    return jax.shard_map(local, mesh=fine, in_specs=in_specs, out_specs=out_specs, check_vma=False)
```

```python
import functools

import jax
import jax.numpy as jnp
from jax import lax
from jax.experimental import pallas as pl
from jax.experimental.pallas import tpu as pltpu
from jax.sharding import Mesh, PartitionSpec as P

F32 = jnp.float32
BF16 = jnp.bfloat16
NEG = 7
ROWS = 88
PADDED = 96
FEAT = 1024
TOTAL = 8 * ROWS
QUARTER = 2 * ROWS
WIDE = 768
LAST = 640
SCALE = 4096 ** (-0.5)
MIB = 1024 * 1024
NT = (((1,), (1,)), ((), ()))
NN = (((1,), (0,)), ((), ()))
TN = (((0,), (0,)), ((), ()))
HBM = pl.BlockSpec(memory_space=pltpu.HBM)
VMEM = pl.BlockSpec(memory_space=pltpu.VMEM)
PIECES = ((0, 0), (1, 0), (2, 0), (3, 0), (4, 0), (4, 48), (5, 0), (6, 0), (7, 0))


def shift(x, axis, count, step):
    return lax.ppermute(x, axis, [(i, (i + step) % count) for i in range(count)])


def gather_z(x):
    half = PADDED // 2
    r1 = shift(x, "z", 8, 1)
    l1 = shift(x, "z", 8, -1)
    r2 = shift(r1, "z", 8, 1)
    l2 = shift(l1, "z", 8, -1)
    r3 = shift(r2, "z", 8, 1)
    l3 = shift(l2, "z", 8, -1)
    r4 = shift(r3[:half], "z", 8, 1)
    l4 = shift(l3[half:], "z", 8, -1)
    return [x, r1, r2, r3, r4, l4, l3, l2, l1]


def position(*axes):
    return tuple(lax.axis_index(a) for a in axes)


def dot(a, b, dims):
    return lax.dot_general(a, b, dims, preferred_element_type=F32)


def in_block(column, b):
    return (column >= b * ROWS) & (column < b * ROWS + ROWS)


def pad_rows(x):
    return jnp.concatenate([x, jnp.zeros((PADDED - ROWS, x.shape[1]), x.dtype)])


def prepare_kernel(q_ref, p_ref, n_ref, owner_ref, row_ref, q_out_ref, out_ref, turn_ref):
    for b in range(8):
        out_ref[b, :, :FEAT] = p_ref[...]
        out_ref[b, :, FEAT:] = n_ref[...]
    q_out_ref[:, :FEAT] = pad_rows(q_ref[...].astype(F32)).astype(BF16)
    lane = lax.broadcasted_iota(jnp.int32, (PADDED, 128), 1).astype(F32)
    turn_ref[...] = jnp.zeros((128, 128), F32)
    turn_ref[:NEG, :ROWS] = owner_ref[...].astype(F32)
    turn_ref[8 : 8 + NEG, :ROWS] = row_ref[...].astype(F32)
    turned = jnp.transpose(turn_ref[...])[:PADDED]
    named = jnp.full((PADDED, 128), -1.0, F32)
    for k in range(NEG):
        named = jnp.where(lane == turned[:, k : k + 1], turned[:, 8 + k : 9 + k], named)
    q_out_ref[:, FEAT:] = named.astype(BF16)


def join_kernel(*refs):
    z = lax.axis_index("z")
    for ref, (k, first) in zip(refs[:9], PIECES):
        row = pl.multiple_of(lax.rem(z + 8 - k, 8) * PADDED + first, 16)
        refs[9][pl.ds(row, ref.shape[0]), :] = ref[...]


def mask_parts(z):
    owner = lax.broadcasted_iota(jnp.int32, (128, TOTAL), 0)
    column = lax.broadcasted_iota(jnp.int32, (128, TOTAL), 1)
    here = (owner < 64) & (((owner >> 1) & 7) == z)
    spot = (owner >> 4) * 2 + (owner & 1)
    spread = jnp.where(here & in_block(column, spot), 1.0, 0.0).astype(BF16)
    inner = column[:8]
    for b in range(1, 8):
        inner = inner - jnp.where(column[:8] >= b * ROWS, ROWS, 0)
    return spread, inner[:1].astype(F32), here, spot


def score_kernel(give, q_ref, pn_ref, out_ref):
    z, xh, core = position("z", "xh", "c")
    half = 1 - core if give else core
    mine = pl.ds(pl.multiple_of(half * 4 * PADDED, 4 * PADDED), 4 * PADDED)
    q, names = q_ref[mine, :FEAT], q_ref[mine, FEAT:]
    spread, inner, here, spot = mask_parts(z)
    mask = dot(names, spread, NN) == inner
    named = jnp.where(mask, dot(q, pn_ref[:, FEAT:], NT), 0.0)
    row = lax.broadcasted_iota(jnp.int32, (TOTAL, 128), 0)
    lane = lax.broadcasted_iota(jnp.int32, (TOTAL, 128), 1)
    gather = jnp.where((lane < 16) & in_block(row, lane & 7), 1.0, 0.0)
    value = lax.dot_general(
        named, gather, NN, precision=lax.Precision.HIGHEST, preferred_element_type=F32
    )
    lane_b = lax.broadcasted_iota(jnp.int32, (128, 128), 1)
    pick = here[:, :128] & (spot[:, :128] == (lane_b & 7)) & (lane_b < 16)
    at_block = dot(names, jnp.where(pick, 1.0, 0.0).astype(BF16), NN)
    tail = jnp.where((at_block >= 0.0) & (lane[: 4 * PADDED] < 16), value, -jnp.inf)
    scores = dot(q, pn_ref[:, :FEAT], NT)
    for t in range(4):
        slot = pl.ds(jnp.where(xh == t // 2, 0, 1), 1)
        rows = slice(t % 2 * ROWS, (t % 2 + 1) * ROWS)
        here_t = slice(t * PADDED, t * PADDED + ROWS)
        out_ref[slot, rows, :TOTAL] = scores[None, here_t]
        out_ref[slot, rows, TOTAL:] = tail[None, here_t, : WIDE - TOTAL]


def soft_kernel(keep_ref, near_ref, far_ref, e_ref, stats_ref, turn_ref):
    y, z, xl, xh, core = position("y", "z", "xl", "xh", "c")
    stats_ref[...] = jnp.zeros(stats_ref.shape, F32)
    column = lax.broadcasted_iota(jnp.int32, (ROWS, WIDE), 1)
    row = lax.broadcasted_iota(jnp.int32, (ROWS, WIDE), 0)
    once = column < TOTAL + 8
    diagonal = column == row + (y * 2 + xl) * ROWS
    lane = lax.broadcasted_iota(jnp.int32, (ROWS, 128), 1)
    for h in range(2):
        rows = slice(h * ROWS, (h + 1) * ROWS)
        scores = (keep_ref[0, rows, :] + near_ref[0, rows, :] + far_ref[0, rows, :]) * SCALE
        peak = jnp.max(scores, axis=1, keepdims=True)
        e = jnp.exp(scores - peak)
        e_ref[rows, :] = e
        part = jnp.sum(jnp.where(once, e, 0.0), axis=1, keepdims=True)
        own = diagonal & (core * 4 + xh * 2 + h == z)
        positive = jnp.sum(jnp.where(own, scores, 0.0), axis=1, keepdims=True)
        info = jnp.where(lane == 0, peak, jnp.where(lane == 1, part, positive))
        turn_ref[...] = jnp.zeros((128, 128), F32)
        turn_ref[:ROWS, :] = info
        turned = jnp.transpose(turn_ref[...])
        for v in range(3):
            at = 2 * v + h
            stats_ref[:, at : at + 1, :] = jnp.broadcast_to(turned[None, v : v + 1], (8, 1, 128))


def settle_kernel(stats_ref, e_ref, out_ref, turn_ref):
    y, z, xl, xh, core = position("y", "z", "xl", "xh", "c")
    every = stats_ref[...]
    own = stats_ref[pl.ds(z, 1)][0]
    top = jnp.max(every[:, 0:2, :], axis=0)
    whole = jnp.sum(every[:, 2:4, :] * jnp.exp(every[:, 0:2, :] - top[None]), axis=0)
    log_total = top + jnp.log(whole)
    valid = lax.broadcasted_iota(jnp.int32, (2, 128), 1) < ROWS
    loss = log_total - own[4:6]
    turn_ref[...] = jnp.zeros((128, 128), F32)
    turn_ref[0:2, :] = jnp.where(valid, jnp.exp(own[0:2] - log_total), 0.0)
    turn_ref[2:4, :] = jnp.where(valid, loss, 0.0)
    turned = jnp.transpose(turn_ref[...])[:ROWS]
    column = lax.broadcasted_iota(jnp.int32, (ROWS, WIDE), 1)
    row = lax.broadcasted_iota(jnp.int32, (ROWS, WIDE), 0)
    diagonal = column == row + (y * 2 + xl) * ROWS
    parts = []
    for h in range(2):
        weight = e_ref[h * ROWS : (h + 1) * ROWS, :] * turned[:, h : h + 1]
        loss_h = turned[:, 2 + h : 3 + h]
        mine = diagonal & (core * 4 + xh * 2 + h == z)
        weight = jnp.where(mine, 0.0, weight)
        high = weight.astype(BF16).astype(F32)
        weight = jnp.where(column < TOTAL + 8, high, weight - high)
        loss_a = loss_h.astype(BF16).astype(F32)
        loss_b = (loss_h - loss_a).astype(BF16).astype(F32)
        weight = jnp.where(column == TOTAL + 16, loss_a, weight)
        weight = jnp.where(column == TOTAL + 17, loss_b, weight)
        weight = jnp.where(column == TOTAL + 18, loss_h - loss_a - loss_b, weight)
        parts.append(pad_rows(weight))
    out_ref[...] = jnp.concatenate(parts).astype(BF16)


def weight_kernel(
    e0_ref, e1_ref, e2_ref, e3_ref, pn_ref, q_ref,
    out_ref, gq_ref, loss_ref, diagonal_ref, w_ref, named_ref, turn_ref,
):
    y, z, xl, xh, core = position("y", "z", "xl", "xh", "c")
    lane = lax.broadcasted_iota(jnp.int32, (128, TOTAL), 0) - (TOTAL - LAST)
    wide = lax.broadcasted_iota(jnp.int32, (128, TOTAL), 1)
    spread = (lane >= 0) & (lane < 8) & in_block(wide, lane)
    spread = jnp.where(spread, 1.0, 0.0).astype(BF16)
    names, inner, _, _ = mask_parts(z)
    turn_ref[...] = jnp.zeros((128, 128), F32)

    def body(e_ref, quarter):
        rows = slice(quarter * 2 * PADDED, (quarter + 1) * 2 * PADDED)
        w_ref[rows, :] = e_ref[:, :TOTAL]
        mask = dot(q_ref[rows, FEAT:], names, NN) == inner
        value = dot(e_ref[:, LAST:], spread, NN)
        named_ref[rows, :] = jnp.where(mask, value, 0.0).astype(BF16)
        for h in range(2):

            @pl.when(z == 2 * quarter + h)
            def _(h=h):
                turn_ref[:PADDED, :] = e_ref[h * PADDED : (h + 1) * PADDED, LAST:].astype(F32)

    parts = ((e0_ref, 0, 0), (e1_ref, 1, 0), (e2_ref, 0, 1), (e3_ref, 1, 1))
    for e_ref, a, b in parts:
        for quarter in range(4):
            here = (core == (quarter // 2 ^ a)) & (xh == (quarter % 2 ^ b))
            pl.when(here)(functools.partial(body, e_ref, quarter))

    gq = dot(w_ref[...], pn_ref[:, :FEAT], NN) + dot(named_ref[...], pn_ref[:, FEAT:], NN)
    gq = SCALE * gq
    for b in range(8):
        gq_ref[b] = gq[b * PADDED : b * PADDED + ROWS].astype(BF16)
    first = TOTAL + 16 - LAST
    loss = jnp.sum(turn_ref[:PADDED, first : first + 3], axis=1, keepdims=True)
    weight = jnp.exp(-loss) - 1.0
    diagonal_ref[...] = jnp.broadcast_to(weight, (PADDED, 128))
    own = pl.ds(pl.multiple_of(z * PADDED, 16), PADDED)
    column = lax.broadcasted_iota(jnp.int32, (PADDED, TOTAL), 1)
    row = lax.broadcasted_iota(jnp.int32, (PADDED, TOTAL), 0)
    here = (column == row + (y * 2 + xl) * ROWS) & (row < ROWS)
    w_ref[own, :] = jnp.where(here, weight, w_ref[own, :].astype(F32)).astype(BF16)
    q = q_ref[:, :FEAT]
    out_ref[:, :FEAT] = (SCALE * dot(w_ref[...], q, TN)).astype(BF16)
    out_ref[:, FEAT:] = (SCALE * dot(named_ref[...], q, TN)).astype(BF16)
    turned = jnp.transpose(turn_ref[...])
    loss = turned[first : first + 1] + turned[first + 1 : first + 2] + turned[first + 2 : first + 3]
    loss_ref[...] = jnp.broadcast_to(loss, (8, 128))


def finish_kernel(gq_ref, diagonal_ref, p_ref, x_ref, gq_out_ref, gp_out_ref, gn_out_ref):
    own = SCALE * diagonal_ref[:ROWS, :1] * p_ref[...].astype(F32)
    gq_out_ref[...] = (gq_ref[...].astype(F32) + own).astype(BF16)
    for first, out_ref in ((0, gp_out_ref), (FEAT, gn_out_ref)):
        total = x_ref[0, :, first : first + FEAT].astype(F32)
        for b in range(1, 8):
            total += x_ref[b, :, first : first + FEAT].astype(F32)
        out_ref[...] = total.astype(BF16)


def shaped(shape, dtype):
    return jax.ShapeDtypeStruct(shape, dtype)


def block(shape):
    return pl.BlockSpec(shape, lambda i: (0,) * len(shape))


def call(kernel, name, operands, outs, scratch=(), far_in=0, far_out=(), limit=20):
    return pl.pallas_call(
        kernel,
        out_shape=outs,
        in_specs=[VMEM] * (len(operands) - far_in) + [HBM] * far_in,
        out_specs=tuple(HBM if i in far_out else VMEM for i in range(len(outs))),
        scratch_shapes=scratch,
        compiler_params=pltpu.CompilerParams(vmem_limit_bytes=limit * MIB),
        cost_estimate=pl.CostEstimate(flops=0, bytes_accessed=1024, transcendentals=0),
        name=name,
    )(*operands)


def blocked(kernel, name, operands, in_specs, outs, scratch=(), limit=60):
    return pl.pallas_call(
        kernel,
        out_shape=outs,
        grid=(1,),
        in_specs=in_specs,
        out_specs=tuple(block(s.shape) for s in outs),
        scratch_shapes=scratch,
        compiler_params=pltpu.CompilerParams(vmem_limit_bytes=limit * MIB),
        name=name,
    )(*operands)


def local(queries, passages, negatives, neg_owner, neg_row):
    plane = ("y", "xl")
    packed, spread = blocked(
        prepare_kernel, "prepare", (queries, passages, negatives, neg_owner.T, neg_row.T),
        [block((ROWS, FEAT))] * 3 + [block((NEG, ROWS))] * 2,
        (shaped((PADDED, FEAT + 128), BF16), shaped((8, ROWS, 2 * FEAT), BF16)),
        scratch=[pltpu.VMEM((128, 128), F32)],
    )
    pn = lax.all_to_all(spread, plane, 0, 0, tiled=True).reshape(TOTAL, 2 * FEAT)
    pieces = gather_z(packed)

    q_cat = call(join_kernel, "join", pieces, (shaped((8 * PADDED, FEAT + 128), BF16),))[0]

    def scores_half(give):
        return call(
            functools.partial(score_kernel, give), "scores_give" if give else "scores_keep",
            (q_cat, pn), (shaped((2, QUARTER, WIDE), F32),),
        )[0]

    give = scores_half(True)
    near = shift(give, "c", 2, 1)
    keep = scores_half(False)
    far = shift(keep[1:] + near[1:], "xh", 2, 1)

    e, stats = call(
        soft_kernel, "soft", (keep, near, far),
        (shaped((QUARTER, WIDE), F32), shaped((8, 8, 128), F32)), [pltpu.VMEM((128, 128), F32)],
    )
    stats = lax.all_to_all(stats, "z", 0, 0, tiled=True)
    e0 = call(
        settle_kernel, "settle", (stats, e), (shaped((2 * PADDED, WIDE), BF16),),
        [pltpu.VMEM((128, 128), F32)],
    )[0]
    e2 = shift(e0, "xh", 2, 1)
    e1 = shift(e0, "c", 2, 1)
    e3 = shift(e2, "c", 2, 1)

    gpn, gq, loss, diagonal = call(
        weight_kernel, "weights", (e0, e1, e2, e3, pn, q_cat),
        (
            shaped((TOTAL, 2 * FEAT), BF16), shaped((8, ROWS, FEAT), BF16),
            shaped((8, 128), F32), shaped((PADDED, 128), F32),
        ),
        [pltpu.VMEM((8 * PADDED, TOTAL), BF16)] * 2 + [pltpu.VMEM((128, 128), F32)],
        limit=24,
    )
    grad_queries = lax.psum_scatter(gq, "z", scatter_dimension=0, tiled=True)[0]
    gpn = lax.all_to_all(gpn.reshape(8, ROWS, 2 * FEAT), plane, 0, 0, tiled=True)
    grads = blocked(
        finish_kernel, "finish", (grad_queries, diagonal, passages, gpn),
        [block((ROWS, FEAT)), block((PADDED, 128)), block((ROWS, FEAT)), VMEM],
        (shaped((ROWS, FEAT), BF16),) * 3, limit=20,
    )
    return (loss[0, :ROWS],) + tuple(grads)


def solution(mesh):
    fine = Mesh(mesh.devices.reshape(4, 8, 2, 2, 2), ("y", "z", "xl", "xh", "c"))
    dp, width = ("y", "z", "xl"), ("xh", "c")
    in_specs = (P(dp, width), P(dp, width), P(dp, width), P(dp, None), P(dp, None))
    out_specs = (P(dp), P(dp, width), P(dp, width), P(dp, width))
    return jax.shard_map(local, mesh=fine, in_specs=in_specs, out_specs=out_specs, check_vma=False)
```

```python
import functools

import jax
import jax.numpy as jnp
from jax import lax
from jax.experimental import pallas as pl
from jax.experimental.pallas import tpu as pltpu
from jax.sharding import Mesh, PartitionSpec as P

F32 = jnp.float32
BF16 = jnp.bfloat16
NEG = 7
ROWS = 88
PADDED = 96
FEAT = 1024
TOTAL = 8 * ROWS
QUARTER = 2 * ROWS
WIDE = 768
LAST = 640
SCALE = 4096 ** (-0.5)
MIB = 1024 * 1024
NT = (((1,), (1,)), ((), ()))
NN = (((1,), (0,)), ((), ()))
TN = (((0,), (0,)), ((), ()))
HBM = pl.BlockSpec(memory_space=pltpu.HBM)
VMEM = pl.BlockSpec(memory_space=pltpu.VMEM)
PIECES = ((0, 0), (1, 0), (2, 0), (3, 0), (4, 0), (4, 48), (5, 0), (6, 0), (7, 0))


def shift(x, axis, count, step):
    return lax.ppermute(x, axis, [(i, (i + step) % count) for i in range(count)])


def gather_z(x):
    half = PADDED // 2
    r1 = shift(x, "z", 8, 1)
    l1 = shift(x, "z", 8, -1)
    r2 = shift(r1, "z", 8, 1)
    l2 = shift(l1, "z", 8, -1)
    r3 = shift(r2, "z", 8, 1)
    l3 = shift(l2, "z", 8, -1)
    r4 = shift(r3[:half], "z", 8, 1)
    l4 = shift(l3[half:], "z", 8, -1)
    return [x, r1, r2, r3, r4, l4, l3, l2, l1]


def position(*axes):
    return tuple(lax.axis_index(a) for a in axes)


def dot(a, b, dims):
    return lax.dot_general(a, b, dims, preferred_element_type=F32)


def in_block(column, b):
    return (column >= b * ROWS) & (column < b * ROWS + ROWS)


def pad_rows(x):
    return jnp.concatenate([x, jnp.zeros((PADDED - ROWS, x.shape[1]), x.dtype)])


def spread_kernel(p_ref, n_ref, out_ref):
    for b in range(out_ref.shape[0]):
        out_ref[b, :, :FEAT] = p_ref[...]
        out_ref[b, :, FEAT:] = n_ref[...]


def pack_kernel(q_ref, owner_ref, row_ref, q_out_ref, turn_ref):
    q_out_ref[:, :FEAT] = pad_rows(q_ref[...].astype(F32)).astype(BF16)
    lane = lax.broadcasted_iota(jnp.int32, (PADDED, 128), 1).astype(F32)
    turn_ref[...] = jnp.zeros((128, 128), F32)
    turn_ref[:NEG, :ROWS] = owner_ref[...].astype(F32)
    turn_ref[8 : 8 + NEG, :ROWS] = row_ref[...].astype(F32)
    turned = jnp.transpose(turn_ref[...])[:PADDED]
    named = jnp.full((PADDED, 128), -1.0, F32)
    for k in range(NEG):
        named = jnp.where(lane == turned[:, k : k + 1], turned[:, 8 + k : 9 + k], named)
    q_out_ref[:, FEAT:] = named.astype(BF16)


def join_kernel(*refs):
    z = lax.axis_index("z")
    for ref, (k, first) in zip(refs[:9], PIECES):
        row = pl.multiple_of(lax.rem(z + 8 - k, 8) * PADDED + first, 16)
        refs[9][pl.ds(row, ref.shape[0]), :] = ref[...]


def mask_parts(z):
    owner = lax.broadcasted_iota(jnp.int32, (128, TOTAL), 0)
    column = lax.broadcasted_iota(jnp.int32, (128, TOTAL), 1)
    here = (owner < 64) & (((owner >> 1) & 7) == z)
    spot = (owner >> 4) * 2 + (owner & 1)
    spread = jnp.where(here & in_block(column, spot), 1.0, 0.0).astype(BF16)
    inner = column[:8]
    for b in range(1, 8):
        inner = inner - jnp.where(column[:8] >= b * ROWS, ROWS, 0)
    return spread, inner[:1].astype(F32), here, spot


def score_kernel(give, q_ref, pn_ref, out_ref):
    z, xh, core = position("z", "xh", "c")
    half = 1 - core if give else core
    mine = pl.ds(pl.multiple_of(half * 4 * PADDED, 4 * PADDED), 4 * PADDED)
    q, names = q_ref[mine, :FEAT], q_ref[mine, FEAT:]
    spread, inner, here, spot = mask_parts(z)
    mask = dot(names, spread, NN) == inner
    named = jnp.where(mask, dot(q, pn_ref[:, FEAT:], NT), 0.0)
    row = lax.broadcasted_iota(jnp.int32, (TOTAL, 128), 0)
    lane = lax.broadcasted_iota(jnp.int32, (TOTAL, 128), 1)
    gather = jnp.where((lane < 16) & in_block(row, lane & 7), 1.0, 0.0)
    value = lax.dot_general(
        named, gather, NN, precision=lax.Precision.HIGHEST, preferred_element_type=F32
    )
    lane_b = lax.broadcasted_iota(jnp.int32, (128, 128), 1)
    pick = here[:, :128] & (spot[:, :128] == (lane_b & 7)) & (lane_b < 16)
    at_block = dot(names, jnp.where(pick, 1.0, 0.0).astype(BF16), NN)
    tail = jnp.where((at_block >= 0.0) & (lane[: 4 * PADDED] < 16), value, -jnp.inf)
    scores = dot(q, pn_ref[:, :FEAT], NT)
    for t in range(4):
        slot = pl.ds(jnp.where(xh == t // 2, 0, 1), 1)
        rows = slice(t % 2 * ROWS, (t % 2 + 1) * ROWS)
        here_t = slice(t * PADDED, t * PADDED + ROWS)
        out_ref[slot, rows, :TOTAL] = scores[None, here_t]
        out_ref[slot, rows, TOTAL:] = tail[None, here_t, : WIDE - TOTAL]


def soft_kernel(keep_ref, near_ref, far_ref, e_ref, stats_ref, turn_ref):
    y, z, xl, xh, core = position("y", "z", "xl", "xh", "c")
    stats_ref[...] = jnp.zeros(stats_ref.shape, F32)
    column = lax.broadcasted_iota(jnp.int32, (ROWS, WIDE), 1)
    row = lax.broadcasted_iota(jnp.int32, (ROWS, WIDE), 0)
    once = column < TOTAL + 8
    diagonal = column == row + (y * 2 + xl) * ROWS
    lane = lax.broadcasted_iota(jnp.int32, (ROWS, 128), 1)
    for h in range(2):
        rows = slice(h * ROWS, (h + 1) * ROWS)
        scores = (keep_ref[0, rows, :] + near_ref[0, rows, :] + far_ref[0, rows, :]) * SCALE
        peak = jnp.max(scores, axis=1, keepdims=True)
        e = jnp.exp(scores - peak)
        e_ref[rows, :] = e
        part = jnp.sum(jnp.where(once, e, 0.0), axis=1, keepdims=True)
        own = diagonal & (core * 4 + xh * 2 + h == z)
        positive = jnp.sum(jnp.where(own, scores, 0.0), axis=1, keepdims=True)
        info = jnp.where(lane == 0, peak, jnp.where(lane == 1, part, positive))
        turn_ref[...] = jnp.zeros((128, 128), F32)
        turn_ref[:ROWS, :] = info
        turned = jnp.transpose(turn_ref[...])
        for v in range(3):
            at = 2 * v + h
            stats_ref[:, at : at + 1, :] = jnp.broadcast_to(turned[None, v : v + 1], (8, 1, 128))


def settle_kernel(stats_ref, e_ref, out_ref, turn_ref):
    y, z, xl, xh, core = position("y", "z", "xl", "xh", "c")
    every = stats_ref[...]
    own = stats_ref[pl.ds(z, 1)][0]
    top = jnp.max(every[:, 0:2, :], axis=0)
    whole = jnp.sum(every[:, 2:4, :] * jnp.exp(every[:, 0:2, :] - top[None]), axis=0)
    log_total = top + jnp.log(whole)
    valid = lax.broadcasted_iota(jnp.int32, (2, 128), 1) < ROWS
    loss = log_total - own[4:6]
    turn_ref[...] = jnp.zeros((128, 128), F32)
    turn_ref[0:2, :] = jnp.where(valid, jnp.exp(own[0:2] - log_total), 0.0)
    turn_ref[2:4, :] = jnp.where(valid, loss, 0.0)
    turned = jnp.transpose(turn_ref[...])[:ROWS]
    column = lax.broadcasted_iota(jnp.int32, (ROWS, WIDE), 1)
    row = lax.broadcasted_iota(jnp.int32, (ROWS, WIDE), 0)
    diagonal = column == row + (y * 2 + xl) * ROWS
    parts = []
    for h in range(2):
        weight = e_ref[h * ROWS : (h + 1) * ROWS, :] * turned[:, h : h + 1]
        loss_h = turned[:, 2 + h : 3 + h]
        mine = diagonal & (core * 4 + xh * 2 + h == z)
        weight = jnp.where(mine, 0.0, weight)
        high = weight.astype(BF16).astype(F32)
        weight = jnp.where(column < TOTAL + 8, high, weight - high)
        loss_a = loss_h.astype(BF16).astype(F32)
        loss_b = (loss_h - loss_a).astype(BF16).astype(F32)
        weight = jnp.where(column == TOTAL + 16, loss_a, weight)
        weight = jnp.where(column == TOTAL + 17, loss_b, weight)
        weight = jnp.where(column == TOTAL + 18, loss_h - loss_a - loss_b, weight)
        parts.append(pad_rows(weight))
    out_ref[...] = jnp.concatenate(parts).astype(BF16)


def weight_kernel(
    e0_ref, e1_ref, e2_ref, e3_ref, pn_ref, q_ref,
    out_ref, gq_ref, loss_ref, diagonal_ref, w_ref, named_ref, turn_ref,
):
    y, z, xl, xh, core = position("y", "z", "xl", "xh", "c")
    lane = lax.broadcasted_iota(jnp.int32, (128, TOTAL), 0) - (TOTAL - LAST)
    wide = lax.broadcasted_iota(jnp.int32, (128, TOTAL), 1)
    spread = (lane >= 0) & (lane < 8) & in_block(wide, lane)
    spread = jnp.where(spread, 1.0, 0.0).astype(BF16)
    names, inner, _, _ = mask_parts(z)
    turn_ref[...] = jnp.zeros((128, 128), F32)

    def body(e_ref, quarter):
        rows = slice(quarter * 2 * PADDED, (quarter + 1) * 2 * PADDED)
        w_ref[rows, :] = e_ref[:, :TOTAL]
        mask = dot(q_ref[rows, FEAT:], names, NN) == inner
        value = dot(e_ref[:, LAST:], spread, NN)
        named_ref[rows, :] = jnp.where(mask, value, 0.0).astype(BF16)
        for h in range(2):

            @pl.when(z == 2 * quarter + h)
            def _(h=h):
                turn_ref[:PADDED, :] = e_ref[h * PADDED : (h + 1) * PADDED, LAST:].astype(F32)

    parts = ((e0_ref, 0, 0), (e1_ref, 1, 0), (e2_ref, 0, 1), (e3_ref, 1, 1))
    for e_ref, a, b in parts:
        for quarter in range(4):
            here = (core == (quarter // 2 ^ a)) & (xh == (quarter % 2 ^ b))
            pl.when(here)(functools.partial(body, e_ref, quarter))

    gq = dot(w_ref[...], pn_ref[:, :FEAT], NN) + dot(named_ref[...], pn_ref[:, FEAT:], NN)
    gq = SCALE * gq
    for b in range(8):
        gq_ref[b] = gq[b * PADDED : b * PADDED + ROWS].astype(BF16)
    first = TOTAL + 16 - LAST
    loss = jnp.sum(turn_ref[:PADDED, first : first + 3], axis=1, keepdims=True)
    weight = jnp.exp(-loss) - 1.0
    diagonal_ref[...] = jnp.broadcast_to(weight, (PADDED, 128))
    own = pl.ds(pl.multiple_of(z * PADDED, 16), PADDED)
    column = lax.broadcasted_iota(jnp.int32, (PADDED, TOTAL), 1)
    row = lax.broadcasted_iota(jnp.int32, (PADDED, TOTAL), 0)
    here = (column == row + (y * 2 + xl) * ROWS) & (row < ROWS)
    w_ref[own, :] = jnp.where(here, weight, w_ref[own, :].astype(F32)).astype(BF16)
    q = q_ref[:, :FEAT]
    out_ref[:, :FEAT] = (SCALE * dot(w_ref[...], q, TN)).astype(BF16)
    out_ref[:, FEAT:] = (SCALE * dot(named_ref[...], q, TN)).astype(BF16)
    turned = jnp.transpose(turn_ref[...])
    loss = turned[first : first + 1] + turned[first + 1 : first + 2] + turned[first + 2 : first + 3]
    loss_ref[...] = jnp.broadcast_to(loss, (8, 128))


def finish_kernel(gq_ref, diagonal_ref, p_ref, x_ref, gq_out_ref, gp_out_ref, gn_out_ref):
    own = SCALE * diagonal_ref[:ROWS, :1] * p_ref[...].astype(F32)
    gq_out_ref[...] = (gq_ref[...].astype(F32) + own).astype(BF16)
    for first, out_ref in ((0, gp_out_ref), (FEAT, gn_out_ref)):
        total = x_ref[0, :, first : first + FEAT].astype(F32)
        for b in range(1, 8):
            total += x_ref[b, :, first : first + FEAT].astype(F32)
        out_ref[...] = total.astype(BF16)


def shaped(shape, dtype):
    return jax.ShapeDtypeStruct(shape, dtype)


def block(shape):
    return pl.BlockSpec(shape, lambda i: (0,) * len(shape))


def call(kernel, name, operands, outs, scratch=(), far_in=0, far_out=(), limit=20):
    return pl.pallas_call(
        kernel,
        out_shape=outs,
        in_specs=[VMEM] * (len(operands) - far_in) + [HBM] * far_in,
        out_specs=tuple(HBM if i in far_out else VMEM for i in range(len(outs))),
        scratch_shapes=scratch,
        compiler_params=pltpu.CompilerParams(vmem_limit_bytes=limit * MIB),
        cost_estimate=pl.CostEstimate(flops=0, bytes_accessed=1024, transcendentals=0),
        name=name,
    )(*operands)


def blocked(kernel, name, operands, in_specs, outs, scratch=(), limit=60):
    return pl.pallas_call(
        kernel,
        out_shape=outs,
        grid=(1,),
        in_specs=in_specs,
        out_specs=tuple(block(s.shape) for s in outs),
        scratch_shapes=scratch,
        compiler_params=pltpu.CompilerParams(vmem_limit_bytes=limit * MIB),
        name=name,
    )(*operands)


def local(queries, passages, negatives, neg_owner, neg_row):
    plane = ("y", "xl")
    spread = pl.pallas_call(
        spread_kernel,
        out_shape=shaped((8, ROWS, 2 * FEAT), BF16),
        grid=(1,),
        in_specs=[block((ROWS, FEAT))] * 2,
        out_specs=pl.BlockSpec((8, ROWS, 2 * FEAT), lambda i: (i, 0, 0)),
        compiler_params=pltpu.CompilerParams(vmem_limit_bytes=60 * MIB),
        name="spread",
    )(passages, negatives)
    queries, spread = lax.optimization_barrier((queries, spread))
    packed = blocked(
        pack_kernel, "prepare", (queries, neg_owner.T, neg_row.T),
        [block((ROWS, FEAT))] + [block((NEG, ROWS))] * 2,
        (shaped((PADDED, FEAT + 128), BF16),), scratch=[pltpu.VMEM((128, 128), F32)],
    )[0]
    pn = lax.all_to_all(spread, plane, 0, 0, tiled=True).reshape(TOTAL, 2 * FEAT)
    pieces = gather_z(packed)

    q_cat = call(join_kernel, "join", pieces, (shaped((8 * PADDED, FEAT + 128), BF16),))[0]

    def scores_half(give):
        return call(
            functools.partial(score_kernel, give), "scores_give" if give else "scores_keep",
            (q_cat, pn), (shaped((2, QUARTER, WIDE), F32),),
        )[0]

    give = scores_half(True)
    near = shift(give, "c", 2, 1)
    keep = scores_half(False)
    far = shift(keep[1:] + near[1:], "xh", 2, 1)

    e, stats = call(
        soft_kernel, "soft", (keep, near, far),
        (shaped((QUARTER, WIDE), F32), shaped((8, 8, 128), F32)), [pltpu.VMEM((128, 128), F32)],
    )
    stats = lax.all_to_all(stats, "z", 0, 0, tiled=True)
    e0 = call(
        settle_kernel, "settle", (stats, e), (shaped((2 * PADDED, WIDE), BF16),),
        [pltpu.VMEM((128, 128), F32)],
    )[0]
    e2 = shift(e0, "xh", 2, 1)
    e1 = shift(e0, "c", 2, 1)
    e3 = shift(e2, "c", 2, 1)

    gpn, gq, loss, diagonal = call(
        weight_kernel, "weights", (e0, e1, e2, e3, pn, q_cat),
        (
            shaped((TOTAL, 2 * FEAT), BF16), shaped((8, ROWS, FEAT), BF16),
            shaped((8, 128), F32), shaped((PADDED, 128), F32),
        ),
        [pltpu.VMEM((8 * PADDED, TOTAL), BF16)] * 2 + [pltpu.VMEM((128, 128), F32)],
        limit=24,
    )
    grad_queries = lax.psum_scatter(gq, "z", scatter_dimension=0, tiled=True)[0]
    gpn = lax.all_to_all(gpn.reshape(8, ROWS, 2 * FEAT), plane, 0, 0, tiled=True)
    grads = blocked(
        finish_kernel, "finish", (grad_queries, diagonal, passages, gpn),
        [block((ROWS, FEAT)), block((PADDED, 128)), block((ROWS, FEAT)), VMEM],
        (shaped((ROWS, FEAT), BF16),) * 3, limit=20,
    )
    return (loss[0, :ROWS],) + tuple(grads)


def solution(mesh):
    fine = Mesh(mesh.devices.reshape(4, 8, 2, 2, 2), ("y", "z", "xl", "xh", "c"))
    dp, width = ("y", "z", "xl"), ("xh", "c")
    in_specs = (P(dp, width), P(dp, width), P(dp, width), P(dp, None), P(dp, None))
    out_specs = (P(dp), P(dp, width), P(dp, width), P(dp, width))
    return jax.shard_map(local, mesh=fine, in_specs=in_specs, out_specs=out_specs, check_vma=False)
```

```python
import functools

import jax
import jax.numpy as jnp
from jax import lax
from jax.experimental import pallas as pl
from jax.experimental.pallas import tpu as pltpu
from jax.sharding import Mesh, PartitionSpec as P

F32 = jnp.float32
BF16 = jnp.bfloat16
NEG = 7
ROWS = 88
PADDED = 96
FEAT = 1024
TOTAL = 8 * ROWS
QUARTER = 2 * ROWS
WIDE = 768
LAST = 640
SCALE = 4096 ** (-0.5)
MIB = 1024 * 1024
NT = (((1,), (1,)), ((), ()))
NN = (((1,), (0,)), ((), ()))
TN = (((0,), (0,)), ((), ()))
HBM = pl.BlockSpec(memory_space=pltpu.HBM)
VMEM = pl.BlockSpec(memory_space=pltpu.VMEM)
PIECES = ((0, 0), (1, 0), (2, 0), (3, 0), (4, 0), (4, 48), (5, 0), (6, 0), (7, 0))


def shift(x, axis, count, step):
    return lax.ppermute(x, axis, [(i, (i + step) % count) for i in range(count)])


def gather_z(x):
    half = PADDED // 2
    r1 = shift(x, "z", 8, 1)
    l1 = shift(x, "z", 8, -1)
    r2 = shift(r1, "z", 8, 1)
    l2 = shift(l1, "z", 8, -1)
    r3 = shift(r2, "z", 8, 1)
    l3 = shift(l2, "z", 8, -1)
    r4 = shift(r3[:half], "z", 8, 1)
    l4 = shift(l3[half:], "z", 8, -1)
    return [x, r1, r2, r3, r4, l4, l3, l2, l1]


def position(*axes):
    return tuple(lax.axis_index(a) for a in axes)


def dot(a, b, dims):
    return lax.dot_general(a, b, dims, preferred_element_type=F32)


def in_block(column, b):
    return (column >= b * ROWS) & (column < b * ROWS + ROWS)


def pad_rows(x):
    return jnp.concatenate([x, jnp.zeros((PADDED - ROWS, x.shape[1]), x.dtype)])


def prepare_kernel(q_ref, p_ref, n_ref, owner_ref, row_ref, q_out_ref, out_ref, turn_ref):
    for b in range(8):
        out_ref[b, :, :FEAT] = p_ref[...]
        out_ref[b, :, FEAT:] = n_ref[...]
    q_out_ref[:, :FEAT] = pad_rows(q_ref[...].astype(F32)).astype(BF16)
    lane = lax.broadcasted_iota(jnp.int32, (PADDED, 128), 1).astype(F32)
    turn_ref[...] = jnp.zeros((128, 128), F32)
    turn_ref[:NEG, :ROWS] = owner_ref[...].astype(F32)
    turn_ref[8 : 8 + NEG, :ROWS] = row_ref[...].astype(F32)
    turned = jnp.transpose(turn_ref[...])[:PADDED]
    named = jnp.full((PADDED, 128), -1.0, F32)
    for k in range(NEG):
        named = jnp.where(lane == turned[:, k : k + 1], turned[:, 8 + k : 9 + k], named)
    q_out_ref[:, FEAT:] = named.astype(BF16)


def join_kernel(*refs):
    z = lax.axis_index("z")
    for ref, (k, first) in zip(refs[:9], PIECES):
        row = pl.multiple_of(lax.rem(z + 8 - k, 8) * PADDED + first, 16)
        refs[9][pl.ds(row, ref.shape[0]), :] = ref[...]


def mask_parts(z):
    owner = lax.broadcasted_iota(jnp.int32, (128, TOTAL), 0)
    column = lax.broadcasted_iota(jnp.int32, (128, TOTAL), 1)
    here = (owner < 64) & (((owner >> 1) & 7) == z)
    spot = (owner >> 4) * 2 + (owner & 1)
    spread = jnp.where(here & in_block(column, spot), 1.0, 0.0).astype(BF16)
    inner = column[:8]
    for b in range(1, 8):
        inner = inner - jnp.where(column[:8] >= b * ROWS, ROWS, 0)
    return spread, inner[:1].astype(F32), here, spot


def score_kernel(give, q_ref, pn_ref, out_ref):
    z, xh, core = position("z", "xh", "c")
    half = 1 - core if give else core
    mine = pl.ds(pl.multiple_of(half * 4 * PADDED, 4 * PADDED), 4 * PADDED)
    q, names = q_ref[mine, :FEAT], q_ref[mine, FEAT:]
    spread, inner, here, spot = mask_parts(z)
    mask = dot(names, spread, NN) == inner
    named = jnp.where(mask, dot(q, pn_ref[:, FEAT:], NT), 0.0)
    row = lax.broadcasted_iota(jnp.int32, (TOTAL, 128), 0)
    lane = lax.broadcasted_iota(jnp.int32, (TOTAL, 128), 1)
    gather = jnp.where((lane < 16) & in_block(row, lane & 7), 1.0, 0.0)
    value = lax.dot_general(
        named, gather, NN, precision=lax.Precision.HIGHEST, preferred_element_type=F32
    )
    lane_b = lax.broadcasted_iota(jnp.int32, (128, 128), 1)
    pick = here[:, :128] & (spot[:, :128] == (lane_b & 7)) & (lane_b < 16)
    at_block = dot(names, jnp.where(pick, 1.0, 0.0).astype(BF16), NN)
    tail = jnp.where((at_block >= 0.0) & (lane[: 4 * PADDED] < 16), value, -jnp.inf)
    scores = dot(q, pn_ref[:, :FEAT], NT)
    for t in range(4):
        slot = pl.ds(jnp.where(xh == t // 2, 0, 1), 1)
        rows = slice(t % 2 * ROWS, (t % 2 + 1) * ROWS)
        here_t = slice(t * PADDED, t * PADDED + ROWS)
        out_ref[slot, rows, :TOTAL] = scores[None, here_t]
        out_ref[slot, rows, TOTAL:] = tail[None, here_t, : WIDE - TOTAL]


def soft_kernel(keep_ref, near_ref, far_ref, e_ref, stats_ref, turn_ref):
    y, z, xl, xh, core = position("y", "z", "xl", "xh", "c")
    stats_ref[...] = jnp.zeros(stats_ref.shape, F32)
    column = lax.broadcasted_iota(jnp.int32, (ROWS, WIDE), 1)
    row = lax.broadcasted_iota(jnp.int32, (ROWS, WIDE), 0)
    once = column < TOTAL + 8
    diagonal = column == row + (y * 2 + xl) * ROWS
    lane = lax.broadcasted_iota(jnp.int32, (ROWS, 128), 1)
    for h in range(2):
        rows = slice(h * ROWS, (h + 1) * ROWS)
        scores = (keep_ref[0, rows, :] + near_ref[0, rows, :] + far_ref[0, rows, :]) * SCALE
        peak = jnp.max(scores, axis=1, keepdims=True)
        e = jnp.exp(scores - peak)
        e_ref[rows, :] = e
        part = jnp.sum(jnp.where(once, e, 0.0), axis=1, keepdims=True)
        own = diagonal & (core * 4 + xh * 2 + h == z)
        positive = jnp.sum(jnp.where(own, scores, 0.0), axis=1, keepdims=True)
        info = jnp.where(lane == 0, peak, jnp.where(lane == 1, part, positive))
        turn_ref[...] = jnp.zeros((128, 128), F32)
        turn_ref[:ROWS, :] = info
        turned = jnp.transpose(turn_ref[...])
        for v in range(3):
            at = 2 * v + h
            stats_ref[:, at : at + 1, :] = jnp.broadcast_to(turned[None, v : v + 1], (8, 1, 128))


def settle_kernel(stats_ref, e_ref, out_ref, turn_ref):
    y, z, xl, xh, core = position("y", "z", "xl", "xh", "c")
    every = stats_ref[...]
    own = stats_ref[pl.ds(z, 1)][0]
    top = jnp.max(every[:, 0:2, :], axis=0)
    whole = jnp.sum(every[:, 2:4, :] * jnp.exp(every[:, 0:2, :] - top[None]), axis=0)
    log_total = top + jnp.log(whole)
    valid = lax.broadcasted_iota(jnp.int32, (2, 128), 1) < ROWS
    loss = log_total - own[4:6]
    turn_ref[...] = jnp.zeros((128, 128), F32)
    turn_ref[0:2, :] = jnp.where(valid, jnp.exp(own[0:2] - log_total), 0.0)
    turn_ref[2:4, :] = jnp.where(valid, loss, 0.0)
    turned = jnp.transpose(turn_ref[...])[:ROWS]
    column = lax.broadcasted_iota(jnp.int32, (ROWS, WIDE), 1)
    row = lax.broadcasted_iota(jnp.int32, (ROWS, WIDE), 0)
    diagonal = column == row + (y * 2 + xl) * ROWS
    parts = []
    for h in range(2):
        weight = e_ref[h * ROWS : (h + 1) * ROWS, :] * turned[:, h : h + 1]
        loss_h = turned[:, 2 + h : 3 + h]
        mine = diagonal & (core * 4 + xh * 2 + h == z)
        weight = jnp.where(mine, 0.0, weight)
        high = weight.astype(BF16).astype(F32)
        weight = jnp.where(column < TOTAL + 8, high, weight - high)
        loss_a = loss_h.astype(BF16).astype(F32)
        loss_b = (loss_h - loss_a).astype(BF16).astype(F32)
        weight = jnp.where(column == TOTAL + 16, loss_a, weight)
        weight = jnp.where(column == TOTAL + 17, loss_b, weight)
        weight = jnp.where(column == TOTAL + 18, loss_h - loss_a - loss_b, weight)
        parts.append(pad_rows(weight))
    out_ref[...] = jnp.concatenate(parts).astype(BF16)


def weight_kernel(
    e0_ref, e1_ref, e2_ref, e3_ref, pn_ref, q_ref,
    out_ref, gq_ref, loss_ref, diagonal_ref, w_ref, named_ref, turn_ref,
):
    y, z, xl, xh, core = position("y", "z", "xl", "xh", "c")
    lane = lax.broadcasted_iota(jnp.int32, (128, TOTAL), 0) - (TOTAL - LAST)
    wide = lax.broadcasted_iota(jnp.int32, (128, TOTAL), 1)
    spread = (lane >= 0) & (lane < 8) & in_block(wide, lane)
    spread = jnp.where(spread, 1.0, 0.0).astype(BF16)
    names, inner, _, _ = mask_parts(z)
    turn_ref[...] = jnp.zeros((128, 128), F32)

    def body(e_ref, quarter):
        rows = slice(quarter * 2 * PADDED, (quarter + 1) * 2 * PADDED)
        w_ref[rows, :] = e_ref[:, :TOTAL]
        mask = dot(q_ref[rows, FEAT:], names, NN) == inner
        value = dot(e_ref[:, LAST:], spread, NN)
        named_ref[rows, :] = jnp.where(mask, value, 0.0).astype(BF16)
        for h in range(2):

            @pl.when(z == 2 * quarter + h)
            def _(h=h):
                turn_ref[:PADDED, :] = e_ref[h * PADDED : (h + 1) * PADDED, LAST:].astype(F32)

    parts = ((e0_ref, 0, 0), (e1_ref, 1, 0), (e2_ref, 0, 1), (e3_ref, 1, 1))
    for e_ref, a, b in parts:
        for quarter in range(4):
            here = (core == (quarter // 2 ^ a)) & (xh == (quarter % 2 ^ b))
            pl.when(here)(functools.partial(body, e_ref, quarter))

    gq = dot(w_ref[...], pn_ref[:, :FEAT], NN) + dot(named_ref[...], pn_ref[:, FEAT:], NN)
    gq = SCALE * gq
    for b in range(8):
        gq_ref[b] = gq[b * PADDED : b * PADDED + ROWS].astype(BF16)
    first = TOTAL + 16 - LAST
    loss = jnp.sum(turn_ref[:PADDED, first : first + 3], axis=1, keepdims=True)
    weight = jnp.exp(-loss) - 1.0
    diagonal_ref[...] = jnp.broadcast_to(weight, (PADDED, 128))
    own = pl.ds(pl.multiple_of(z * PADDED, 16), PADDED)
    column = lax.broadcasted_iota(jnp.int32, (PADDED, TOTAL), 1)
    row = lax.broadcasted_iota(jnp.int32, (PADDED, TOTAL), 0)
    here = (column == row + (y * 2 + xl) * ROWS) & (row < ROWS)
    w_ref[own, :] = jnp.where(here, weight, w_ref[own, :].astype(F32)).astype(BF16)
    q = q_ref[:, :FEAT]
    out_ref[:, :FEAT] = (SCALE * dot(w_ref[...], q, TN)).astype(BF16)
    out_ref[:, FEAT:] = (SCALE * dot(named_ref[...], q, TN)).astype(BF16)
    turned = jnp.transpose(turn_ref[...])
    loss = turned[first : first + 1] + turned[first + 1 : first + 2] + turned[first + 2 : first + 3]
    loss_ref[...] = jnp.broadcast_to(loss, (8, 128))


def finish_kernel(gq_ref, diagonal_ref, p_ref, x_ref, gq_out_ref, gp_out_ref, gn_out_ref):
    own = SCALE * diagonal_ref[:ROWS, :1] * p_ref[...].astype(F32)
    gq_out_ref[...] = (gq_ref[...].astype(F32) + own).astype(BF16)
    for first, out_ref in ((0, gp_out_ref), (FEAT, gn_out_ref)):
        total = x_ref[0, :, first : first + FEAT].astype(F32)
        for b in range(1, 8):
            total += x_ref[b, :, first : first + FEAT].astype(F32)
        out_ref[...] = total.astype(BF16)


def shaped(shape, dtype):
    return jax.ShapeDtypeStruct(shape, dtype)


def block(shape):
    return pl.BlockSpec(shape, lambda i: (0,) * len(shape))


def call(kernel, name, operands, outs, scratch=(), far_in=0, far_out=(), limit=20):
    return pl.pallas_call(
        kernel,
        out_shape=outs,
        in_specs=[VMEM] * (len(operands) - far_in) + [HBM] * far_in,
        out_specs=tuple(HBM if i in far_out else VMEM for i in range(len(outs))),
        scratch_shapes=scratch,
        compiler_params=pltpu.CompilerParams(vmem_limit_bytes=limit * MIB),
        cost_estimate=pl.CostEstimate(flops=0, bytes_accessed=1024, transcendentals=0),
        name=name,
    )(*operands)


def blocked(kernel, name, operands, in_specs, outs, scratch=(), limit=60):
    return pl.pallas_call(
        kernel,
        out_shape=outs,
        grid=(1,),
        in_specs=in_specs,
        out_specs=tuple(block(s.shape) for s in outs),
        scratch_shapes=scratch,
        compiler_params=pltpu.CompilerParams(vmem_limit_bytes=limit * MIB),
        name=name,
    )(*operands)


def local(queries, passages, negatives, neg_owner, neg_row):
    plane = ("y", "xl")
    packed, spread = blocked(
        prepare_kernel, "prepare", (queries, passages, negatives, neg_owner.T, neg_row.T),
        [block((ROWS, FEAT))] * 3 + [block((NEG, ROWS))] * 2,
        (shaped((PADDED, FEAT + 128), BF16), shaped((8, ROWS, 2 * FEAT), BF16)),
        scratch=[pltpu.VMEM((128, 128), F32)],
    )
    pn = lax.all_to_all(spread, plane, 0, 0, tiled=True).reshape(TOTAL, 2 * FEAT)
    pieces = gather_z(packed)

    q_cat = call(join_kernel, "join", pieces, (shaped((8 * PADDED, FEAT + 128), BF16),))[0]

    def scores_half(give):
        return call(
            functools.partial(score_kernel, give), "scores_give" if give else "scores_keep",
            (q_cat, pn), (shaped((2, QUARTER, WIDE), F32),),
        )[0]

    give = scores_half(True)
    near = shift(give, "c", 2, 1)
    keep = scores_half(False)
    far = shift(keep[1:] + near[1:], "xh", 2, 1)

    e, stats = call(
        soft_kernel, "soft", (keep, near, far),
        (shaped((QUARTER, WIDE), F32), shaped((8, 8, 128), F32)), [pltpu.VMEM((128, 128), F32)],
    )
    stats = lax.all_to_all(stats, "z", 0, 0, tiled=True)
    e0 = call(
        settle_kernel, "settle", (stats, e), (shaped((2 * PADDED, WIDE), BF16),),
        [pltpu.VMEM((128, 128), F32)],
    )[0]
    e2 = shift(e0, "xh", 2, 1)
    e0, e2 = lax.optimization_barrier((e0, e2))
    e1 = shift(e0, "c", 2, 1)
    e3 = shift(e2, "c", 2, 1)

    gpn, gq, loss, diagonal = call(
        weight_kernel, "weights", (e0, e1, e2, e3, pn, q_cat),
        (
            shaped((TOTAL, 2 * FEAT), BF16), shaped((8, ROWS, FEAT), BF16),
            shaped((8, 128), F32), shaped((PADDED, 128), F32),
        ),
        [pltpu.VMEM((8 * PADDED, TOTAL), BF16)] * 2 + [pltpu.VMEM((128, 128), F32)],
        limit=24,
    )
    grad_queries = lax.psum_scatter(gq, "z", scatter_dimension=0, tiled=True)[0]
    gpn = lax.all_to_all(gpn.reshape(8, ROWS, 2 * FEAT), plane, 0, 0, tiled=True)
    grads = blocked(
        finish_kernel, "finish", (grad_queries, diagonal, passages, gpn),
        [block((ROWS, FEAT)), block((PADDED, 128)), block((ROWS, FEAT)), VMEM],
        (shaped((ROWS, FEAT), BF16),) * 3, limit=20,
    )
    return (loss[0, :ROWS],) + tuple(grads)


def solution(mesh):
    fine = Mesh(mesh.devices.reshape(4, 8, 2, 2, 2), ("y", "z", "xl", "xh", "c"))
    dp, width = ("y", "z", "xl"), ("xh", "c")
    in_specs = (P(dp, width), P(dp, width), P(dp, width), P(dp, None), P(dp, None))
    out_specs = (P(dp), P(dp, width), P(dp, width), P(dp, width))
    return jax.shard_map(local, mesh=fine, in_specs=in_specs, out_specs=out_specs, check_vma=False)
```
